512 devices in a mesh: ctx: 8 (over y), exp: 64 (over x, z, core).
Axes of the slice: x: 4, y: 8, z: 8, core: 2. Of those that a mesh axis runs over, the one named last changes fastest.
Arguments:
- hidden_rows: bfloat16 [65536, 1440], P(('ctx', 'exp')), may hold values from -6 to 6
- queries: bfloat16 [65536, 2048], P(('ctx', 'exp')), may hold values from -7 to 7
- keys: bfloat16 [65536, 256], P(('ctx', 'exp')), may hold values from -7 to 7
- values: bfloat16 [65536, 256], P(('ctx', 'exp')), may hold values from -6 to 6
- sinks: float32 [32], replicated, may hold values from 0 to 5
- norm_gain: float32 [1440], replicated, may hold values from 0.1 to 1.9
- learner_row: int32 [65536], P(('ctx', 'exp')), may hold values from 0 to 65535, as said below
- expert_ids: int32 [65536, 2], P(('ctx', 'exp')), may hold values from 0 to 63, all different within a row; in each aligned block of 128 rows (0 to 127, 128 to 255, ...) at most 8 rows name the same one
- route_weight: float32 [65536, 2], P(('ctx', 'exp')), may hold values from 0.1 to 1
- gate_w: bfloat16 [64, 1440, 1440], P('exp', 'ctx'), may hold values from -0.15625 to 0.15625
- up_w: bfloat16 [64, 1440, 1440], P('exp', 'ctx'), may hold values from -0.15625 to 0.15625
- down_w: bfloat16 [64, 1440, 1440], P('exp', 'ctx'), may hold values from -0.15625 to 0.15625
Outputs:
- attn_rows: bfloat16 [65536, 2048], P(('ctx', 'exp'))
- mixed: bfloat16 [65536, 1440], P(('ctx', 'exp'))
The draws below stay inside these ranges and needn't reach their ends.
Inputs may be any that keep to these rules, and one draw needn't show every extreme that they name: `learner_row`: A permutation of the rows. Every row stays within its block of 8192 rows; within such a block, the learner rows of device d of a block whose offset within d's 128 rows lies in [s * 2, (s + 1) * 2) come from the rollout rows of device s of that block. `expert_ids`: each row names 2 different experts. Among the 128 rows of one device no expert is named more than 8 times; some device names some expert exactly 8 times.
All inputs are finite; a program needn't handle non-finite values.
Results may differ from the reference program's by a relative error of at most 0.0053.
Values may be sent and summed in bfloat16 or wider, within the bound.
No kernel may reach another device: no remote copies, remote signals or barrier semaphores. Data moves between devices by JAX's collectives and lax.ppermute only.
A program may use at most 128 MiB of HBM per device.

```python
import math
import jax
import jax.numpy as jnp
import numpy as np
from jax import lax

D = 1440
FFW = 1440
QHEADS = 32
KVHEADS = 4
HEAD = 64
WINDOW = 128
ROUTES = 2
TOK_DEV = 128
EXPERTS = 64
CAP = 8
TOKENS = 65536


def shuffle_rows(subkey):
    return jax.random.permutation(subkey, TOK_DEV)


def rollout_targets(key):
    base = jax.random.fold_in(key, 101)
    senders = TOKENS // TOK_DEV
    per_peer = TOK_DEV // EXPERTS
    shuffled = jax.vmap(shuffle_rows)(jax.random.split(base, senders)).astype(jnp.int32)
    sender = jnp.arange(senders, dtype=jnp.int32)[:, None]
    group_start = sender // EXPERTS * (EXPERTS * TOK_DEV)
    within = sender % EXPERTS
    target = group_start + shuffled // per_peer * TOK_DEV + within * per_peer + shuffled % per_peer
    return target.reshape(-1).astype(jnp.int32)


def draw_learner_row(key, part):
    return rollout_targets(key)


def draw_queries(key, part):
    key = jax.random.fold_in(key, 7)
    drawn = jnp.clip(1.5 * jax.random.normal(key, (TOKENS, QHEADS * HEAD), jnp.float32), -7.0, 7.0)
    return drawn.astype(jnp.bfloat16)


def draw_keys(key, part):
    key = jax.random.fold_in(key, 13)
    drawn = jnp.clip(1.5 * jax.random.normal(key, (TOKENS, KVHEADS * HEAD), jnp.float32), -7.0, 7.0)
    return drawn.astype(jnp.bfloat16)


def steps_of(rng, dims, shards, low, largest):
    loudness = 1.0
    for dim, blocks in shards:
        steps = jax.random.uniform(jax.random.fold_in(jax.random.fold_in(rng, 6), dim), (blocks,), jnp.float32, low / len(shards), largest / len(shards))
        loudness = loudness * jnp.repeat(jnp.exp(steps), dims[dim] // blocks).reshape((-1,) + (1,) * (len(dims) - 1 - dim))
    return loudness


def deal_out(key, own, number, rows, amount, top, most, skew):
    ranking = jax.random.permutation(key, amount)
    crowded, ordinary = load_shares(amount, rows * top, most, skew, True), load_shares(amount, rows * top, most, skew, False)
    places = jnp.arange(amount)

    def named(sizes, offset_by):
        used = int((sizes > 0).sum())
        fixed = max(1, used // 4)
        passed = fixed + (places - fixed + offset_by * (used - fixed)) % max(1, amount - fixed)
        return jnp.zeros((amount,), jnp.int32).at[ranking[jnp.where(places < fixed, places, passed)]].set(jnp.asarray(sizes, jnp.int32))

    sizes = jnp.where(number % 4 == 0, named(crowded, number // 4), named(ordinary, number - number // 4 - 1))
    mixed = jax.random.permutation(jax.random.fold_in(own, 3), amount)
    giver, sink = mixed[0:amount // 2 * 2:2], mixed[1:amount // 2 * 2:2]
    slack = jnp.minimum(sizes[giver] - 1, most - sizes[sink]) // 2
    slack = jnp.where((giver == ranking[0]) | (sink == ranking[0]) | (sizes[sink] == 0), 0, jnp.maximum(slack, 0))
    passed = jax.random.randint(jax.random.fold_in(own, 4), (amount // 2,), 0, 1 << 20) % (slack + 1)
    sizes = sizes.at[giver].add(-passed).at[sink].add(passed)
    items = jnp.searchsorted(jnp.cumsum(sizes), jnp.arange(rows * top), side="right").astype(jnp.int32)
    listing = items.reshape(top, rows).T
    listing = listing[jax.random.permutation(jax.random.fold_in(own, 1), rows)]
    offset_by = jax.random.randint(jax.random.fold_in(own, 2), (rows, 1), 0, top)
    return jnp.take_along_axis(listing, (jnp.arange(top)[None, :] + offset_by) % top, axis=1)


def load_shares(number_of, total, limit, slope, full):
    weights = [(1 << 20) // math.isqrt(standing ** slope) + 1 for standing in range(1, number_of + 1)]
    largest = limit if full else min(limit, max(-(-total // number_of), total * weights[0] // sum(weights)))
    least = 1 if total - largest >= number_of - 1 else 0
    holding, surplus = [largest] + [least] * (number_of - 1), total - largest - least * (number_of - 1)
    while surplus > 0:
        movable = [i for i in range(1, number_of) if holding[i] < largest] or [i for i in range(1, number_of) if holding[i] < limit]
        mass, budget = sum([weights[i] for i in movable]), surplus
        for i in movable:
            extra = min(limit - holding[i], max(1, budget * weights[i] // mass), surplus)
            holding[i] = holding[i] + extra
            surplus = surplus - extra
    return np.array(holding)


def centred(key, dims, spread, most, cuts=(), kind=jnp.bfloat16):
    factor_of = steps_of(key, dims, cuts, -0.22, 0.18) if cuts else 1.0
    entries = jax.random.normal(key, dims, jnp.float32) * spread * factor_of
    return jnp.minimum(jnp.maximum(entries, -most), most).astype(kind)


def setup_inputs(seed: int = 0) -> dict:
    streams_of = jax.random.split(jax.random.key(seed), 13)
    hidden_rows = centred(streams_of[0], (TOKENS, D), 1.0, 6.0, ((0, 512),))
    queries = draw_queries(jax.random.fold_in(streams_of[12], 71), 0)
    keys = draw_keys(jax.random.fold_in(streams_of[12], 71), 0)
    values = centred(streams_of[3], (TOKENS, KVHEADS * HEAD), 1.0, 6.0, ((0, 512),))
    sinks = jnp.clip(jax.random.uniform(streams_of[4], (QHEADS,), jnp.float32, 0.0, 5.0), 0.0, 5.0)
    norm_gain = jnp.clip(1.0 + 0.18 * jax.random.normal(streams_of[5], (D,), jnp.float32), 0.1, 1.9)
    learner_row = draw_learner_row(jax.random.fold_in(streams_of[12], 71), 0)
    expert_ids_keys = jax.random.split(jax.random.fold_in(streams_of[7], 1), TOKENS // TOK_DEV)
    expert_ids_turns = jax.random.permutation(jax.random.fold_in(streams_of[7], 3), TOKENS // TOK_DEV)
    expert_ids = jax.vmap(lambda own, number: deal_out(jax.random.fold_in(streams_of[7], 2), own, number, TOK_DEV, EXPERTS, ROUTES, CAP, 2))(expert_ids_keys, expert_ids_turns).reshape((TOKENS, ROUTES))
    route_weight = jnp.clip(0.1 + 0.9 * jax.random.uniform(streams_of[8], (TOKENS, ROUTES), jnp.float32) ** steps_of(streams_of[8], (TOKENS, ROUTES), ((0, 512),), -0.2, 0.2), 0.1, 1.0)
    gate_w = centred(streams_of[9], (EXPERTS, D, FFW), D ** -0.5, 0.15625, ((0, 64), (1, 8)))
    up_w = centred(streams_of[10], (EXPERTS, D, FFW), D ** -0.5, 0.15625, ((0, 64), (1, 8)))
    down_w = centred(streams_of[11], (EXPERTS, FFW, D), FFW ** -0.5, 0.15625, ((0, 64), (1, 8)))
    return dict(hidden_rows=hidden_rows, queries=queries, keys=keys, values=values, sinks=sinks, norm_gain=norm_gain, learner_row=learner_row, expert_ids=expert_ids, route_weight=route_weight, gate_w=gate_w, up_w=up_w, down_w=down_w)


def relayout(array, learner_row):
    return jnp.zeros_like(array).at[learner_row].set(array)

def attend(query_rows, key_rows, value_rows, sinks):
    groups = QHEADS // KVHEADS
    blocks = TOKENS // WINDOW
    padded_keys = jnp.concatenate([jnp.zeros((WINDOW, key_rows.shape[1]), key_rows.dtype), key_rows], 0)
    padded_values = jnp.concatenate([jnp.zeros((WINDOW, value_rows.shape[1]), value_rows.dtype), value_rows], 0)
    sink_logit = sinks.reshape(KVHEADS, groups)[:, :, None]
    score_scale = 1.0 / math.sqrt(HEAD)

    def one_block(block_index):
        start = (block_index * WINDOW).astype(jnp.int32)
        query_block = lax.dynamic_slice_in_dim(query_rows, start, WINDOW, 0).astype(jnp.float32)
        query_block = query_block.reshape(WINDOW, KVHEADS, groups, HEAD)
        key_block = lax.dynamic_slice_in_dim(padded_keys, start, 2 * WINDOW, 0).astype(jnp.float32)
        key_block = key_block.reshape(2 * WINDOW, KVHEADS, HEAD)
        value_block = lax.dynamic_slice_in_dim(padded_values, start, 2 * WINDOW, 0).astype(jnp.float32)
        value_block = value_block.reshape(2 * WINDOW, KVHEADS, HEAD)
        scores = jnp.einsum('ihgd,jhd->hgij', query_block, key_block) * score_scale
        query_place = start + jnp.arange(WINDOW, dtype=jnp.int32)
        key_place = start - WINDOW + jnp.arange(2 * WINDOW, dtype=jnp.int32)
        distance = query_place[:, None] - key_place[None, :]
        allowed = (distance >= 0) & (distance < WINDOW) & (key_place >= 0)[None, :]
        scores = jnp.where(allowed, scores, -1e+30)
        row_max = jnp.maximum(lax.optimization_barrier(jnp.max(scores, -1)), sink_logit)
        expo_terms = jnp.exp(scores - row_max[..., None])
        denom_total = lax.optimization_barrier(jnp.sum(expo_terms, -1)) + jnp.exp(sink_logit - row_max)
        probs = (expo_terms / denom_total[..., None]).astype(jnp.bfloat16)
        attended = jnp.einsum('hgij,jhd->ihgd', probs.astype(jnp.float32), value_block)
        return attended.reshape(WINDOW, QHEADS * HEAD).astype(jnp.bfloat16)
    outputs = lax.map(one_block, jnp.arange(blocks, dtype=jnp.int32))
    return outputs.reshape(TOKENS, QHEADS * HEAD)

def expert_mix(normed, expert_ids, route_weight, gate_w, up_w, down_w):
    pair_expert = expert_ids.reshape(-1).astype(jnp.int32)
    most_rows = TOKENS // TOK_DEV * CAP
    sorted_pairs = jnp.argsort(pair_expert, stable=True).astype(jnp.int32)
    padded_pairs = jnp.concatenate([sorted_pairs, jnp.zeros((most_rows,), jnp.int32)], 0)
    counts = lax.optimization_barrier(jnp.sum((pair_expert[:, None] == jnp.arange(EXPERTS, dtype=jnp.int32)[None, :]).astype(jnp.int32), 0))
    starts = (jnp.cumsum(counts) - counts).astype(jnp.int32)
    flat_weight = route_weight.reshape(-1)

    def one_expert(totals, expert):
        pair_ids = lax.dynamic_slice_in_dim(padded_pairs, starts[expert], most_rows, 0)
        valid = jnp.arange(most_rows, dtype=jnp.int32) < counts[expert]
        token_ids = pair_ids // ROUTES
        picked = normed[token_ids]
        gate = jnp.dot(picked, gate_w[expert], preferred_element_type=jnp.float32)
        upward = jnp.dot(picked, up_w[expert], preferred_element_type=jnp.float32)
        activ = (gate * jax.nn.sigmoid(1.702 * gate) * (upward + 1.0)).astype(jnp.bfloat16)
        expert_out = jnp.dot(activ, down_w[expert], preferred_element_type=jnp.float32).astype(jnp.bfloat16)
        factor = jnp.where(valid, flat_weight[pair_ids], 0.0)
        totals = totals.at[token_ids].add(expert_out.astype(jnp.float32) * factor[:, None])
        return (totals, None)
    totals, unused = lax.scan(one_expert, jnp.zeros((TOKENS, D), jnp.float32), jnp.arange(EXPERTS, dtype=jnp.int32))
    return totals

def reference(hidden_rows, queries, keys, values, sinks, norm_gain, learner_row, expert_ids, route_weight, gate_w, up_w, down_w):
    resid = relayout(hidden_rows, learner_row)
    query_rows = relayout(queries, learner_row)
    key_rows = relayout(keys, learner_row)
    value_rows = relayout(values, learner_row)
    attn_rows = attend(query_rows, key_rows, value_rows, sinks)
    resid_float = resid.astype(jnp.float32)
    mean_square = lax.optimization_barrier(jnp.mean(resid_float * resid_float, -1, keepdims=True))
    normed = (resid_float * lax.rsqrt(mean_square + 1e-05) * norm_gain).astype(jnp.bfloat16)
    totals = expert_mix(normed, expert_ids, route_weight, gate_w, up_w, down_w)
    mixed = (resid_float + totals).astype(jnp.bfloat16)
    return (attn_rows, mixed)
```

```python
import math

import jax
import jax.numpy as jnp
from jax import lax
from jax.sharding import PartitionSpec as P

D = 1440
FFW = 1440
QHEADS = 32
KVHEADS = 4
HEAD = 64
WINDOW = 128
ROUTES = 2
CAP = 8
MAIN = 1408
DOWN_CUTS = (0, 640, 1440)


def shifted(block, axis, distance):
    devices = range(lax.axis_size(axis))
    route = [(i - distance, i) for i in devices if i - distance in devices]
    return lax.ppermute(block, axis, route)


def pick_rows(choice, rows):
    return jnp.dot(choice, rows, preferred_element_type=jnp.float32).astype(jnp.bfloat16)


def gathered(block):
    rows, columns = block.shape
    pairs = lax.all_gather(block.reshape(rows // 2, 2, columns), "ctx", axis=0, tiled=True)
    return pairs.reshape(-1, columns)


def exchange(rows, peer_count):
    parts = rows.reshape(peer_count, -1, rows.shape[1])
    return lax.all_to_all(parts, "exp", split_axis=0, concat_axis=0, tiled=True).reshape(rows.shape)


def gated_hidden(gate, upward):
    return (gate * jax.nn.sigmoid(1.702 * gate) * (upward + 1.0)).astype(jnp.bfloat16)


def attend(query_rows, key_value_rows, sinks):
    tokens_here = query_rows.shape[0]
    previous = shifted(key_value_rows, ("ctx", "exp"), 1)
    span_rows = WINDOW + tokens_here
    groups = QHEADS // KVHEADS
    span = jnp.concatenate([previous, key_value_rows], 0)
    all_keys = span[:, : KVHEADS * HEAD].reshape(span_rows, KVHEADS, HEAD)
    all_values = span[:, KVHEADS * HEAD :].reshape(span_rows, KVHEADS, HEAD)
    query_heads = query_rows.reshape(tokens_here, KVHEADS, groups, HEAD)
    scores = jnp.einsum(
        "ihgd,jhd->hgij", query_heads, all_keys, preferred_element_type=jnp.float32
    ) * (1.0 / math.sqrt(HEAD))
    first_row = lax.axis_index(("ctx", "exp")) * tokens_here
    query_place = first_row + jnp.arange(tokens_here, dtype=jnp.int32)
    key_place = first_row - WINDOW + jnp.arange(span_rows, dtype=jnp.int32)
    distance = query_place[:, None] - key_place[None, :]
    allowed = (distance >= 0) & (distance < WINDOW) & (key_place >= 0)[None, :]
    scores = jnp.where(allowed, scores, -1e30)
    sink_logit = sinks.reshape(KVHEADS, groups)[:, :, None]
    row_max = jnp.maximum(jnp.max(scores, -1), sink_logit)
    expo_terms = jnp.exp(scores - row_max[..., None])
    denom_total = jnp.sum(expo_terms, -1) + jnp.exp(sink_logit - row_max)
    probs = (expo_terms / denom_total[..., None]).astype(jnp.bfloat16)
    attended = jnp.einsum("hgij,jhd->ihgd", probs, all_values, preferred_element_type=jnp.float32)
    return attended.reshape(tokens_here, QHEADS * HEAD).astype(jnp.bfloat16)


def per_device(
    hidden_rows,
    queries,
    keys,
    values,
    sinks,
    norm_gain,
    learner_row,
    expert_ids,
    route_weight,
    gate_w,
    up_w,
    down_w,
):
    tokens_here = hidden_rows.shape[0]
    peer_count = lax.axis_size("exp")
    per_peer = tokens_here // peer_count
    gate_block, up_block, down_block = gate_w[0], up_w[0], down_w[0]

    wide = jnp.concatenate(
        [
            gate_block[:, :MAIN],
            up_block[:, :MAIN],
            gate_block[:, MAIN:],
            up_block[:, MAIN:],
            down_block[:, MAIN:],
        ],
        1,
    )
    wide = gathered(wide)

    slot = learner_row % (peer_count * tokens_here) // tokens_here * per_peer + learner_row % per_peer
    order = (jnp.arange(tokens_here, dtype=jnp.int32)[:, None] == slot[None, :]).astype(jnp.bfloat16)
    packed = jnp.concatenate([queries, keys, values, hidden_rows], 1)
    arrived = exchange(pick_rows(order, packed), peer_count)
    query_rows = arrived[:, : QHEADS * HEAD]
    key_value_rows = arrived[:, QHEADS * HEAD : (QHEADS + 2 * KVHEADS) * HEAD]
    resid = arrived[:, (QHEADS + 2 * KVHEADS) * HEAD :]

    resid_float = resid.astype(jnp.float32)
    mean_square = jnp.mean(resid_float * resid_float, -1, keepdims=True)
    normed = (resid_float * lax.rsqrt(mean_square + 1e-05) * norm_gain).astype(jnp.bfloat16)

    slots_total = peer_count * CAP
    pair_count = tokens_here * ROUTES
    pair_expert = expert_ids.reshape(-1)
    hits = pair_expert[:, None] == jnp.arange(peer_count, dtype=jnp.int32)[None, :]
    pair_place = jnp.arange(pair_count, dtype=jnp.int32)
    before = (pair_place[:, None] > pair_place[None, :]).astype(jnp.bfloat16)
    earlier = jnp.dot(before, hits.astype(jnp.bfloat16), preferred_element_type=jnp.float32)
    pair_rank = jnp.sum(jnp.where(hits, earlier, 0.0), 1).astype(jnp.int32)
    slot_index = (pair_expert * CAP + pair_rank).reshape(tokens_here, ROUTES)
    slots = jnp.arange(slots_total, dtype=jnp.int32)
    sent = sum(slots[:, None] == slot_index[None, :, r] for r in range(ROUTES))
    expert_rows = exchange(pick_rows(sent.astype(jnp.bfloat16), normed), peer_count)
    weight_high = lax.reduce_precision(route_weight, 8, 7)
    weight_low = route_weight - weight_high

    def selection(weight):
        return sum(
            jnp.where(slots[None, :] == slot_index[:, r, None], weight[:, r, None], 0.0)
            for r in range(ROUTES)
        ).astype(jnp.bfloat16)

    combine = jnp.concatenate([selection(weight_high), selection(weight_low)], 0)

    attn_rows = attend(query_rows, key_value_rows, sinks)

    def project(weight):
        return jnp.dot(expert_rows, weight, preferred_element_type=jnp.float32)

    wide, attn_rows, combine, down_block = lax.optimization_barrier(
        (wide, attn_rows, combine, down_block)
    )
    down_parts = [gathered(down_block[:, : DOWN_CUTS[1]])]
    rest = 2 * MAIN + D - MAIN
    gate = jnp.concatenate([project(wide[:, :MAIN]), project(wide[:, 2 * MAIN : rest])], 1)
    upward = jnp.concatenate(
        [project(wide[:, MAIN : 2 * MAIN]), project(wide[:, rest : 2 * D])], 1
    )
    activ, down_block = lax.optimization_barrier((gated_hidden(gate, upward), down_block))
    down_parts.append(gathered(down_block[:, DOWN_CUTS[1] : MAIN]))
    down_rest = wide[:, 2 * D :]
    mixed_parts = []
    for part, (a, b) in zip(down_parts, zip(DOWN_CUTS, DOWN_CUTS[1:])):
        if b > MAIN:
            part = jnp.concatenate([part, down_rest], 1)
        expert_out = jnp.dot(activ, part, preferred_element_type=jnp.float32).astype(jnp.bfloat16)
        returned = exchange(expert_out, peer_count)
        both = jnp.dot(combine, returned, preferred_element_type=jnp.float32)
        total = both[:tokens_here] + both[tokens_here:]
        mixed_parts.append((resid_float[:, a:b] + total).astype(jnp.bfloat16))
    return (attn_rows, jnp.concatenate(mixed_parts, 1))


def solution(mesh):
    return jax.shard_map(
        per_device,
        mesh=mesh,
        in_specs=(
            P(("ctx", "exp"), None),
            P(("ctx", "exp"), None),
            P(("ctx", "exp"), None),
            P(("ctx", "exp"), None),
            P(),
            P(),
            P(("ctx", "exp")),
            P(("ctx", "exp"), None),
            P(("ctx", "exp"), None),
            P("exp", "ctx", None),
            P("exp", "ctx", None),
            P("exp", "ctx", None),
        ),
        out_specs=(P(("ctx", "exp"), None), P(("ctx", "exp"), None)),
        check_vma=False,
    )
```

```python
import math

import jax
import jax.numpy as jnp
from jax import lax
from jax.experimental import pallas as pl
from jax.experimental.pallas import tpu as pltpu
from jax.sharding import PartitionSpec as P

D = 1440
FFW = 1440
QHEADS = 32
KVHEADS = 4
HEAD = 64
WINDOW = 128
ROUTES = 2
CAP = 8
FIRST = 640
PANELS = ((0, 512), (512, 1024), (1024, 1440))
VMEM_BYTES = 40 * 1024 * 1024


def shifted(block, axis, distance):
    devices = range(lax.axis_size(axis))
    route = [(i - distance, i) for i in devices if i - distance in devices]
    return lax.ppermute(block, axis, route)


def pick_rows(choice, rows):
    return jnp.dot(choice, rows, preferred_element_type=jnp.float32).astype(jnp.bfloat16)


def ring(block, forward_steps):
    count = lax.axis_size("ctx")
    behind, ahead = [block], [block]
    for step in range(max(forward_steps, count - 1 - forward_steps)):
        if step < forward_steps:
            route = [(i, (i + 1) % count) for i in range(count)]
            behind.append(lax.ppermute(behind[-1], "ctx", route))
        if step < count - 1 - forward_steps:
            route = [(i, (i - 1) % count) for i in range(count)]
            ahead.append(lax.ppermute(ahead[-1], "ctx", route))
    return [block] + behind[1:] + ahead[1:]


def ring_owner(forward_steps):
    count = lax.axis_size("ctx")
    shifts = [-step for step in range(forward_steps + 1)]
    shifts += [step for step in range(1, count - forward_steps)]
    return (lax.axis_index("ctx") + jnp.array(shifts, jnp.int32)) % count


def hidden_kernel(owner_ref, rows_ref, gate_ref, *refs):
    up_refs, out_ref, sliced, hidden = refs[:-3], refs[-3], refs[-2], refs[-1]
    count, depth = gate_ref.shape[0], gate_ref.shape[1]
    for s in range(count):
        sliced[s] = rows_ref[:, s * depth : (s + 1) * depth]
    for low, high in PANELS:
        gate = jnp.zeros((rows_ref.shape[0], high - low), jnp.float32)
        upward = jnp.zeros((rows_ref.shape[0], high - low), jnp.float32)
        for s in range(count):
            gate += jnp.dot(
                sliced[s], gate_ref[s, :, low:high], preferred_element_type=jnp.float32
            )
        for s in range(count):
            upward += jnp.dot(
                sliced[owner_ref[s]], up_refs[s][:, low:high], preferred_element_type=jnp.float32
            )
        hidden[:, low:high] = gated_hidden(gate, upward)
    for s in range(count):
        out_ref[s] = hidden[:, s * depth : (s + 1) * depth]


def hidden_call(owner, rows, gate_all, up_blocks):
    count, depth, width = gate_all.shape
    whole = pl.BlockSpec(memory_space=pltpu.VMEM)
    return pl.pallas_call(
        hidden_kernel,
        out_shape=jax.ShapeDtypeStruct((width // depth, rows.shape[0], depth), jnp.bfloat16),
        in_specs=[pl.BlockSpec(memory_space=pltpu.SMEM)] + [whole] * (2 + count),
        out_specs=whole,
        scratch_shapes=[
            pltpu.VMEM((count, rows.shape[0], depth), jnp.bfloat16),
            pltpu.VMEM((rows.shape[0], width), jnp.bfloat16),
        ],
        compiler_params=pltpu.CompilerParams(vmem_limit_bytes=VMEM_BYTES),
        cost_estimate=pl.CostEstimate(
            flops=4 * rows.shape[0] * width * width,
            bytes_accessed=4 * width * width + 4 * rows.shape[0] * width,
            transcendentals=rows.shape[0] * width,
        ),
    )(owner, rows, gate_all, *up_blocks)


def output_kernel(owner_ref, activ_ref, *refs):
    down_refs, out_ref = refs[:-1], refs[-1]
    count = activ_ref.shape[0]
    total = jnp.zeros(out_ref.shape, jnp.float32)
    for s in range(count):
        block = down_refs[0][s] if len(down_refs) == 1 else down_refs[s][...]
        total += jnp.dot(activ_ref[owner_ref[s]], block, preferred_element_type=jnp.float32)
    out_ref[...] = total.astype(jnp.bfloat16)


def output_call(owner, activ, blocks):
    rows, width = activ.shape[1], blocks[0].shape[-1]
    inner = activ.shape[0] * activ.shape[2]
    whole = pl.BlockSpec(memory_space=pltpu.VMEM)
    return pl.pallas_call(
        output_kernel,
        out_shape=jax.ShapeDtypeStruct((rows, width), jnp.bfloat16),
        in_specs=[pl.BlockSpec(memory_space=pltpu.SMEM)] + [whole] * (1 + len(blocks)),
        out_specs=whole,
        compiler_params=pltpu.CompilerParams(vmem_limit_bytes=VMEM_BYTES),
        cost_estimate=pl.CostEstimate(
            flops=2 * rows * width * inner,
            bytes_accessed=2 * (width * inner + rows * inner + rows * width),
            transcendentals=0,
        ),
    )(owner, activ, *blocks)


def exchange(rows, peer_count):
    parts = rows.reshape(peer_count, -1, rows.shape[1])
    return lax.all_to_all(parts, "exp", split_axis=0, concat_axis=0, tiled=True).reshape(rows.shape)


def gated_hidden(gate, upward):
    return (gate * jax.nn.sigmoid(1.702 * gate) * (upward + 1.0)).astype(jnp.bfloat16)


def attend(query_rows, key_value_rows, sinks):
    tokens_here = query_rows.shape[0]
    previous = shifted(key_value_rows, ("ctx", "exp"), 1)
    span_rows = WINDOW + tokens_here
    groups = QHEADS // KVHEADS
    span = jnp.concatenate([previous, key_value_rows], 0)
    all_keys = span[:, : KVHEADS * HEAD].reshape(span_rows, KVHEADS, HEAD)
    all_values = span[:, KVHEADS * HEAD :].reshape(span_rows, KVHEADS, HEAD)
    query_heads = query_rows.reshape(tokens_here, KVHEADS, groups, HEAD)
    scores = jnp.einsum(
        "ihgd,jhd->hgij", query_heads, all_keys, preferred_element_type=jnp.float32
    ) * (1.0 / math.sqrt(HEAD))
    first_row = lax.axis_index(("ctx", "exp")) * tokens_here
    query_place = first_row + jnp.arange(tokens_here, dtype=jnp.int32)
    key_place = first_row - WINDOW + jnp.arange(span_rows, dtype=jnp.int32)
    distance = query_place[:, None] - key_place[None, :]
    allowed = (distance >= 0) & (distance < WINDOW) & (key_place >= 0)[None, :]
    scores = jnp.where(allowed, scores, -1e30)
    sink_logit = sinks.reshape(KVHEADS, groups)[:, :, None]
    row_max = jnp.maximum(jnp.max(scores, -1), sink_logit)
    expo_terms = jnp.exp(scores - row_max[..., None])
    denom_total = jnp.sum(expo_terms, -1) + jnp.exp(sink_logit - row_max)
    probs = (expo_terms / denom_total[..., None]).astype(jnp.bfloat16)
    attended = jnp.einsum("hgij,jhd->ihgd", probs, all_values, preferred_element_type=jnp.float32)
    return attended.reshape(tokens_here, QHEADS * HEAD).astype(jnp.bfloat16)


def per_device(
    hidden_rows,
    queries,
    keys,
    values,
    sinks,
    norm_gain,
    learner_row,
    expert_ids,
    route_weight,
    gate_w,
    up_w,
    down_w,
):
    tokens_here = hidden_rows.shape[0]
    peer_count = lax.axis_size("exp")
    per_peer = tokens_here // peer_count
    gate_block, up_block, down_block = gate_w[0], up_w[0], down_w[0]

    context_count = lax.axis_size("ctx")
    forward = context_count // 2
    gate_all = lax.all_gather(gate_block, "ctx", axis=0)
    up_blocks = ring(up_block, forward)

    slot = learner_row % (peer_count * tokens_here) // tokens_here * per_peer + learner_row % per_peer
    order = (jnp.arange(tokens_here, dtype=jnp.int32)[:, None] == slot[None, :]).astype(jnp.bfloat16)
    resid = exchange(pick_rows(order, hidden_rows), peer_count)
    resid, up_blocks[1], up_blocks[5] = lax.optimization_barrier(
        (resid, up_blocks[1], up_blocks[5])
    )

    resid_float = resid.astype(jnp.float32)
    mean_square = jnp.mean(resid_float * resid_float, -1, keepdims=True)
    normed = (resid_float * lax.rsqrt(mean_square + 1e-05) * norm_gain).astype(jnp.bfloat16)

    slots_total = peer_count * CAP
    pair_count = tokens_here * ROUTES
    pair_expert = expert_ids.reshape(-1)
    hits = pair_expert[:, None] == jnp.arange(peer_count, dtype=jnp.int32)[None, :]
    pair_place = jnp.arange(pair_count, dtype=jnp.int32)
    before = (pair_place[:, None] > pair_place[None, :]).astype(jnp.bfloat16)
    earlier = jnp.dot(before, hits.astype(jnp.bfloat16), preferred_element_type=jnp.float32)
    pair_rank = jnp.sum(jnp.where(hits, earlier, 0.0), 1).astype(jnp.int32)
    slot_index = (pair_expert * CAP + pair_rank).reshape(tokens_here, ROUTES)
    slots = jnp.arange(slots_total, dtype=jnp.int32)
    sent = sum(slots[:, None] == slot_index[None, :, r] for r in range(ROUTES))
    outgoing = pick_rows(sent.astype(jnp.bfloat16), normed)
    outgoing, up_blocks[2], up_blocks[6] = lax.optimization_barrier(
        (outgoing, up_blocks[2], up_blocks[6])
    )
    expert_rows = exchange(outgoing, peer_count)
    packed = jnp.concatenate([queries, keys, values], 1)
    packed, outgoing, gate_all, up_blocks[3], up_blocks[4], up_blocks[7] = (
        lax.optimization_barrier(
            (packed, outgoing, gate_all, up_blocks[3], up_blocks[4], up_blocks[7])
        )
    )
    arrived = exchange(pick_rows(order, packed), peer_count)
    query_rows = arrived[:, : QHEADS * HEAD]
    key_value_rows = arrived[:, QHEADS * HEAD :]
    weight_high = lax.reduce_precision(route_weight, 8, 7)
    weight_low = route_weight - weight_high

    def selection(weight):
        return sum(
            jnp.where(slots[None, :] == slot_index[:, r, None], weight[:, r, None], 0.0)
            for r in range(ROUTES)
        ).astype(jnp.bfloat16)

    combine = jnp.concatenate([selection(weight_high), selection(weight_low)], 0)

    attn_rows = attend(query_rows, key_value_rows, sinks)

    gate_all, down_late = lax.optimization_barrier((gate_all, down_block[:, FIRST:]))
    down_late = lax.all_gather(down_late, "ctx", axis=0)
    up_blocks[3], down_soon = lax.optimization_barrier((up_blocks[3], down_block[:, :FIRST]))
    down_soon = ring(down_soon, context_count - 1 - forward)

    activ = hidden_call(ring_owner(forward), expert_rows, gate_all, up_blocks)
    parts = (
        (0, ring_owner(context_count - 1 - forward), down_soon),
        (FIRST, jnp.arange(context_count, dtype=jnp.int32), [down_late]),
    )
    mixed_parts = []
    for low, owner, blocks in parts:
        expert_out = output_call(owner, activ, blocks)
        returned = exchange(expert_out, peer_count)
        both = jnp.dot(combine, returned, preferred_element_type=jnp.float32)
        total = both[:tokens_here] + both[tokens_here:]
        resid_part = resid_float[:, low : low + total.shape[1]]
        mixed_parts.append((resid_part + total).astype(jnp.bfloat16))
    return (attn_rows, jnp.concatenate(mixed_parts, 1))


def solution(mesh):
    return jax.shard_map(
        per_device,
        mesh=mesh,
        in_specs=(
            P(("ctx", "exp"), None),
            P(("ctx", "exp"), None),
            P(("ctx", "exp"), None),
            P(("ctx", "exp"), None),
            P(),
            P(),
            P(("ctx", "exp")),
            P(("ctx", "exp"), None),
            P(("ctx", "exp"), None),
            P("exp", "ctx", None),
            P("exp", "ctx", None),
            P("exp", "ctx", None),
        ),
        out_specs=(P(("ctx", "exp"), None), P(("ctx", "exp"), None)),
        check_vma=False,
    )
```

```python
import math

import jax
import jax.numpy as jnp
from jax import lax
from jax.experimental import pallas as pl
from jax.experimental.pallas import tpu as pltpu
from jax.sharding import PartitionSpec as P

D = 1440
FFW = 1440
QHEADS = 32
KVHEADS = 4
HEAD = 64
WINDOW = 128
ROUTES = 2
CAP = 8
PANELS = ((0, 512), (512, 1024), (1024, 1440))
VMEM_BYTES = 60 * 1024 * 1024


def shifted(block, axis, distance):
    devices = range(lax.axis_size(axis))
    route = [(i - distance, i) for i in devices if i - distance in devices]
    return lax.ppermute(block, axis, route)


def pick_rows(choice, rows):
    return jnp.dot(choice, rows, preferred_element_type=jnp.float32).astype(jnp.bfloat16)


def ring(block, forward_steps):
    count = lax.axis_size("ctx")
    behind, ahead = [block], [block]
    for step in range(max(forward_steps, count - 1 - forward_steps)):
        if step < forward_steps:
            route = [(i, (i + 1) % count) for i in range(count)]
            behind.append(lax.ppermute(behind[-1], "ctx", route))
        if step < count - 1 - forward_steps:
            route = [(i, (i - 1) % count) for i in range(count)]
            ahead.append(lax.ppermute(ahead[-1], "ctx", route))
    return [block] + behind[1:] + ahead[1:]


def ring_owner(forward_steps):
    count = lax.axis_size("ctx")
    shifts = [-step for step in range(forward_steps + 1)]
    shifts += [step for step in range(1, count - forward_steps)]
    return (lax.axis_index("ctx") + jnp.array(shifts, jnp.int32)) % count


def hidden_kernel(rows_ref, wide_ref, out_ref, sliced, wide, hidden, arrival):
    count, depth = wide_ref.shape[0], wide_ref.shape[2]
    copies = [
        pltpu.make_async_copy(wide_ref.at[s], wide.at[s], arrival.at[s]) for s in range(count)
    ]
    for copy in copies:
        copy.start()
    for s in range(count):
        sliced[s] = rows_ref[:, s * depth : (s + 1) * depth]
    for low, high in PANELS:
        gate = jnp.zeros((rows_ref.shape[0], high - low), jnp.float32)
        upward = jnp.zeros((rows_ref.shape[0], high - low), jnp.float32)
        for s in range(count):
            if low == 0:
                copies[s].wait()
            gate += jnp.dot(
                sliced[s], wide[s, 0, :, low:high], preferred_element_type=jnp.float32
            )
            upward += jnp.dot(
                sliced[s], wide[s, 1, :, low:high], preferred_element_type=jnp.float32
            )
        hidden[:, low:high] = gated_hidden(gate, upward)
    for s in range(count):
        out_ref[s] = hidden[:, s * depth : (s + 1) * depth]


def hidden_call(rows, wide_all):
    count, _, depth, width = wide_all.shape
    whole = pl.BlockSpec(memory_space=pltpu.VMEM)
    return pl.pallas_call(
        hidden_kernel,
        out_shape=jax.ShapeDtypeStruct((width // depth, rows.shape[0], depth), jnp.bfloat16),
        in_specs=[whole, pl.BlockSpec(memory_space=pltpu.HBM)],
        out_specs=whole,
        scratch_shapes=[
            pltpu.VMEM((count, rows.shape[0], depth), jnp.bfloat16),
            pltpu.VMEM(wide_all.shape, jnp.bfloat16),
            pltpu.VMEM((rows.shape[0], width), jnp.bfloat16),
            pltpu.SemaphoreType.DMA((count,)),
        ],
        compiler_params=pltpu.CompilerParams(vmem_limit_bytes=VMEM_BYTES),
        cost_estimate=pl.CostEstimate(
            flops=4 * rows.shape[0] * width * width,
            bytes_accessed=4 * width * width + 4 * rows.shape[0] * width,
            transcendentals=rows.shape[0] * width,
        ),
    )(rows, wide_all)


def output_kernel(owner_ref, activ_ref, *refs):
    count = activ_ref.shape[0]
    out_ref, down, arrival = refs[count:]
    copies = [
        pltpu.make_async_copy(refs[s], down.at[s], arrival.at[s]) for s in range(count)
    ]
    for copy in copies:
        copy.start()
    for low, high in PANELS:
        total = jnp.zeros((out_ref.shape[0], high - low), jnp.float32)
        for s in range(count):
            if low == 0:
                copies[s].wait()
            total += jnp.dot(
                activ_ref[owner_ref[s]], down[s, :, low:high], preferred_element_type=jnp.float32
            )
        out_ref[:, low:high] = total.astype(jnp.bfloat16)


def output_call(owner, activ, blocks):
    count, rows, depth = activ.shape
    width = blocks[0].shape[1]
    whole = pl.BlockSpec(memory_space=pltpu.VMEM)
    return pl.pallas_call(
        output_kernel,
        out_shape=jax.ShapeDtypeStruct((rows, width), jnp.bfloat16),
        in_specs=[pl.BlockSpec(memory_space=pltpu.SMEM), whole]
        + [pl.BlockSpec(memory_space=pltpu.HBM)] * count,
        out_specs=whole,
        scratch_shapes=[
            pltpu.VMEM((count, depth, width), jnp.bfloat16),
            pltpu.SemaphoreType.DMA((count,)),
        ],
        compiler_params=pltpu.CompilerParams(vmem_limit_bytes=VMEM_BYTES),
        cost_estimate=pl.CostEstimate(
            flops=2 * rows * width * count * depth,
            bytes_accessed=2 * (width * count * depth + rows * count * depth + rows * width),
            transcendentals=0,
        ),
    )(owner, activ, *blocks)


def exchange(rows, peer_count):
    parts = rows.reshape(peer_count, -1, rows.shape[1])
    return lax.all_to_all(parts, "exp", split_axis=0, concat_axis=0, tiled=True).reshape(rows.shape)


def gated_hidden(gate, upward):
    return (gate * jax.nn.sigmoid(1.702 * gate) * (upward + 1.0)).astype(jnp.bfloat16)


def attend(query_rows, key_value_rows, sinks):
    tokens_here = query_rows.shape[0]
    previous = shifted(key_value_rows, ("ctx", "exp"), 1)
    span_rows = WINDOW + tokens_here
    groups = QHEADS // KVHEADS
    span = jnp.concatenate([previous, key_value_rows], 0)
    all_keys = span[:, : KVHEADS * HEAD].reshape(span_rows, KVHEADS, HEAD)
    all_values = span[:, KVHEADS * HEAD :].reshape(span_rows, KVHEADS, HEAD)
    query_heads = query_rows.reshape(tokens_here, KVHEADS, groups, HEAD)
    scores = jnp.einsum(
        "ihgd,jhd->hgij", query_heads, all_keys, preferred_element_type=jnp.float32
    ) * (1.0 / math.sqrt(HEAD))
    first_row = lax.axis_index(("ctx", "exp")) * tokens_here
    query_place = first_row + jnp.arange(tokens_here, dtype=jnp.int32)
    key_place = first_row - WINDOW + jnp.arange(span_rows, dtype=jnp.int32)
    distance = query_place[:, None] - key_place[None, :]
    allowed = (distance >= 0) & (distance < WINDOW) & (key_place >= 0)[None, :]
    scores = jnp.where(allowed, scores, -1e30)
    sink_logit = sinks.reshape(KVHEADS, groups)[:, :, None]
    row_max = jnp.maximum(jnp.max(scores, -1), sink_logit)
    expo_terms = jnp.exp(scores - row_max[..., None])
    denom_total = jnp.sum(expo_terms, -1) + jnp.exp(sink_logit - row_max)
    probs = (expo_terms / denom_total[..., None]).astype(jnp.bfloat16)
    attended = jnp.einsum("hgij,jhd->ihgd", probs, all_values, preferred_element_type=jnp.float32)
    return attended.reshape(tokens_here, QHEADS * HEAD).astype(jnp.bfloat16)


def per_device(
    hidden_rows,
    queries,
    keys,
    values,
    sinks,
    norm_gain,
    learner_row,
    expert_ids,
    route_weight,
    gate_w,
    up_w,
    down_w,
):
    tokens_here = hidden_rows.shape[0]
    peer_count = lax.axis_size("exp")
    per_peer = tokens_here // peer_count
    gate_block, up_block, down_block = gate_w[0], up_w[0], down_w[0]

    context_count = lax.axis_size("ctx")
    forward = context_count // 2
    wide = jnp.stack([gate_block, up_block])
    wide, down_block = lax.optimization_barrier((wide, down_block))
    wide_all = lax.all_gather(wide, "ctx", axis=0)
    down_blocks = ring(down_block, forward)

    def after_step(step, value):
        held = [place for place in (step, forward + step) if place < context_count]
        barred = lax.optimization_barrier((value, *[down_blocks[place] for place in held]))
        for place, block in zip(held, barred[1:]):
            down_blocks[place] = block
        return barred[0]

    slot = learner_row % (peer_count * tokens_here) // tokens_here * per_peer + learner_row % per_peer
    order = (jnp.arange(tokens_here, dtype=jnp.int32)[:, None] == slot[None, :]).astype(jnp.bfloat16)
    resid = exchange(pick_rows(order, hidden_rows), peer_count)
    resid = after_step(1, resid)

    resid_float = resid.astype(jnp.float32)
    mean_square = jnp.mean(resid_float * resid_float, -1, keepdims=True)
    normed = (resid_float * lax.rsqrt(mean_square + 1e-05) * norm_gain).astype(jnp.bfloat16)

    slots_total = peer_count * CAP
    pair_count = tokens_here * ROUTES
    pair_expert = expert_ids.reshape(-1)
    hits = pair_expert[:, None] == jnp.arange(peer_count, dtype=jnp.int32)[None, :]
    pair_place = jnp.arange(pair_count, dtype=jnp.int32)
    before = (pair_place[:, None] > pair_place[None, :]).astype(jnp.bfloat16)
    earlier = jnp.dot(before, hits.astype(jnp.bfloat16), preferred_element_type=jnp.float32)
    pair_rank = jnp.sum(jnp.where(hits, earlier, 0.0), 1).astype(jnp.int32)
    slot_index = (pair_expert * CAP + pair_rank).reshape(tokens_here, ROUTES)
    slots = jnp.arange(slots_total, dtype=jnp.int32)
    sent = sum(slots[:, None] == slot_index[None, :, r] for r in range(ROUTES))
    outgoing = pick_rows(sent.astype(jnp.bfloat16), normed)
    expert_rows = exchange(outgoing, peer_count)
    packed = jnp.concatenate([queries, keys, values], 1)
    expert_rows, packed = lax.optimization_barrier((expert_rows, after_step(2, packed)))
    arrived = exchange(pick_rows(order, packed), peer_count)
    query_rows = arrived[:, : QHEADS * HEAD]
    key_value_rows = arrived[:, QHEADS * HEAD :]
    weight_high = lax.reduce_precision(route_weight, 8, 7)
    weight_low = route_weight - weight_high

    def selection(weight):
        return sum(
            jnp.where(slots[None, :] == slot_index[:, r, None], weight[:, r, None], 0.0)
            for r in range(ROUTES)
        ).astype(jnp.bfloat16)

    combine = jnp.concatenate([selection(weight_high), selection(weight_low)], 0)

    attn_rows = attend(query_rows, key_value_rows, sinks)

    activ = hidden_call(expert_rows, wide_all)
    expert_out = output_call(ring_owner(forward), activ, down_blocks)
    returned = exchange(expert_out, peer_count)
    both = jnp.dot(combine, returned, preferred_element_type=jnp.float32)
    total = both[:tokens_here] + both[tokens_here:]
    return (attn_rows, (resid_float + total).astype(jnp.bfloat16))


def solution(mesh):
    return jax.shard_map(
        per_device,
        mesh=mesh,
        in_specs=(
            P(("ctx", "exp"), None),
            P(("ctx", "exp"), None),
            P(("ctx", "exp"), None),
            P(("ctx", "exp"), None),
            P(),
            P(),
            P(("ctx", "exp")),
            P(("ctx", "exp"), None),
            P(("ctx", "exp"), None),
            P("exp", "ctx", None),
            P("exp", "ctx", None),
            P("exp", "ctx", None),
        ),
        out_specs=(P(("ctx", "exp"), None), P(("ctx", "exp"), None)),
        check_vma=False,
    )
```

```python
import math

import jax
import jax.numpy as jnp
from jax import lax
from jax.experimental import pallas as pl
from jax.experimental.pallas import tpu as pltpu
from jax.sharding import PartitionSpec as P

D = 1440
FFW = 1440
QHEADS = 32
KVHEADS = 4
HEAD = 64
WINDOW = 128
ROUTES = 2
CAP = 8
LANES = 128
PANEL = 512
VMEM_BYTES = 60 * 1024 * 1024


def shifted(block, axis, distance):
    devices = range(lax.axis_size(axis))
    route = [(i - distance, i) for i in devices if i - distance in devices]
    return lax.ppermute(block, axis, route)


def pick_rows(choice, rows):
    return jnp.dot(choice, rows, preferred_element_type=jnp.float32).astype(jnp.bfloat16)


def panels(width):
    return [(low, min(low + PANEL, width)) for low in range(0, width, PANEL)]


def experts_kernel(rows_ref, wide_ref, out_ref, sliced, wide, total, hidden, arrival):
    count, depth = wide_ref.shape[0], wide_ref.shape[1]
    width = rows_ref.shape[1]
    copies = [
        pltpu.make_async_copy(wide_ref.at[s], wide.at[s], arrival.at[s]) for s in range(count)
    ]
    for copy in copies:
        copy.start()
    for s in range(count):
        sliced[s] = rows_ref[:, s * depth : (s + 1) * depth]
    for s in range(count):
        copies[s].wait()
        for low, high in panels(total.shape[1]):
            part = jnp.dot(sliced[s], wide[s, :, low:high], preferred_element_type=jnp.float32)
            total[:, low:high] = part if s == 0 else total[:, low:high] + part
    for low, high in panels(width):
        hidden[:, low:high] = gated_hidden(
            total[:, low:high], total[:, width + low : width + high]
        )
    for s in range(count):
        sliced[s] = hidden[:, s * depth : (s + 1) * depth]
    start = 2 * width // LANES * LANES
    for low, high in panels(3 * width - start):
        part = jnp.dot(
            sliced[0], wide[0, :, start + low : start + high], preferred_element_type=jnp.float32
        )
        for s in range(1, count):
            part += jnp.dot(
                sliced[s],
                wide[s, :, start + low : start + high],
                preferred_element_type=jnp.float32,
            )
        total[:, low:high] = part
    lead = 2 * width - start
    out_ref[...] = total[:, lead : lead + width].astype(jnp.bfloat16)


def experts_call(rows, wide_all):
    count, depth, _ = wide_all.shape
    slots, width = rows.shape
    whole = pl.BlockSpec(memory_space=pltpu.VMEM)
    return pl.pallas_call(
        experts_kernel,
        out_shape=jax.ShapeDtypeStruct((slots, width), jnp.bfloat16),
        in_specs=[whole, pl.BlockSpec(memory_space=pltpu.HBM)],
        out_specs=whole,
        scratch_shapes=[
            pltpu.VMEM((count, slots, depth), jnp.bfloat16),
            pltpu.VMEM(wide_all.shape, jnp.bfloat16),
            pltpu.VMEM((slots, -(-2 * width // LANES) * LANES), jnp.float32),
            pltpu.VMEM((slots, width), jnp.bfloat16),
            pltpu.SemaphoreType.DMA((count,)),
        ],
        compiler_params=pltpu.CompilerParams(vmem_limit_bytes=VMEM_BYTES),
        cost_estimate=pl.CostEstimate(
            flops=6 * slots * width * width,
            bytes_accessed=6 * width * width + 4 * slots * width,
            transcendentals=slots * width,
        ),
    )(rows, wide_all)


def exchange(rows, peer_count):
    parts = rows.reshape(peer_count, -1, rows.shape[1])
    return lax.all_to_all(parts, "exp", split_axis=0, concat_axis=0, tiled=True).reshape(rows.shape)


def gated_hidden(gate, upward):
    return (gate * jax.nn.sigmoid(1.702 * gate) * (upward + 1.0)).astype(jnp.bfloat16)


def attend(query_rows, key_value_rows, sinks):
    tokens_here = query_rows.shape[0]
    previous = shifted(key_value_rows, ("ctx", "exp"), 1)
    span_rows = WINDOW + tokens_here
    groups = QHEADS // KVHEADS
    span = jnp.concatenate([previous, key_value_rows], 0)
    all_keys = span[:, : KVHEADS * HEAD].reshape(span_rows, KVHEADS, HEAD)
    all_values = span[:, KVHEADS * HEAD :].reshape(span_rows, KVHEADS, HEAD)
    query_heads = query_rows.reshape(tokens_here, KVHEADS, groups, HEAD)
    scores = jnp.einsum(
        "ihgd,jhd->hgij", query_heads, all_keys, preferred_element_type=jnp.float32
    ) * (1.0 / math.sqrt(HEAD))
    first_row = lax.axis_index(("ctx", "exp")) * tokens_here
    query_place = first_row + jnp.arange(tokens_here, dtype=jnp.int32)
    key_place = first_row - WINDOW + jnp.arange(span_rows, dtype=jnp.int32)
    distance = query_place[:, None] - key_place[None, :]
    allowed = (distance >= 0) & (distance < WINDOW) & (key_place >= 0)[None, :]
    scores = jnp.where(allowed, scores, -1e30)
    sink_logit = sinks.reshape(KVHEADS, groups)[:, :, None]
    row_max = jnp.maximum(jnp.max(scores, -1), sink_logit)
    expo_terms = jnp.exp(scores - row_max[..., None])
    denom_total = jnp.sum(expo_terms, -1) + jnp.exp(sink_logit - row_max)
    probs = (expo_terms / denom_total[..., None]).astype(jnp.bfloat16)
    attended = jnp.einsum("hgij,jhd->ihgd", probs, all_values, preferred_element_type=jnp.float32)
    return attended.reshape(tokens_here, QHEADS * HEAD).astype(jnp.bfloat16)


def per_device(
    hidden_rows,
    queries,
    keys,
    values,
    sinks,
    norm_gain,
    learner_row,
    expert_ids,
    route_weight,
    gate_w,
    up_w,
    down_w,
):
    tokens_here = hidden_rows.shape[0]
    peer_count = lax.axis_size("exp")
    per_peer = tokens_here // peer_count
    gate_block, up_block, down_block = gate_w[0], up_w[0], down_w[0]

    wide_all = lax.all_gather(
        jnp.concatenate([gate_block, up_block, down_block], 1), "ctx", axis=0
    )

    slot = learner_row % (peer_count * tokens_here) // tokens_here * per_peer + learner_row % per_peer
    order = (jnp.arange(tokens_here, dtype=jnp.int32)[:, None] == slot[None, :]).astype(jnp.bfloat16)
    resid = exchange(pick_rows(order, hidden_rows), peer_count)
    resid_float = resid.astype(jnp.float32)
    mean_square = jnp.mean(resid_float * resid_float, -1, keepdims=True)
    normed = (resid_float * lax.rsqrt(mean_square + 1e-05) * norm_gain).astype(jnp.bfloat16)

    slots_total = peer_count * CAP
    pair_count = tokens_here * ROUTES
    pair_expert = expert_ids.reshape(-1)
    hits = pair_expert[:, None] == jnp.arange(peer_count, dtype=jnp.int32)[None, :]
    pair_place = jnp.arange(pair_count, dtype=jnp.int32)
    before = (pair_place[:, None] > pair_place[None, :]).astype(jnp.bfloat16)
    earlier = jnp.dot(before, hits.astype(jnp.bfloat16), preferred_element_type=jnp.float32)
    pair_rank = jnp.sum(jnp.where(hits, earlier, 0.0), 1).astype(jnp.int32)
    slot_index = (pair_expert * CAP + pair_rank).reshape(tokens_here, ROUTES)
    slots = jnp.arange(slots_total, dtype=jnp.int32)
    sent = sum(slots[:, None] == slot_index[None, :, r] for r in range(ROUTES))
    outgoing = pick_rows(sent.astype(jnp.bfloat16), normed)
    expert_rows = exchange(outgoing, peer_count)
    packed = jnp.concatenate([queries, keys, values], 1)
    expert_rows, packed = lax.optimization_barrier((expert_rows, packed))
    arrived = exchange(pick_rows(order, packed), peer_count)
    query_rows = arrived[:, : QHEADS * HEAD]
    key_value_rows = arrived[:, QHEADS * HEAD :]
    weight_high = lax.reduce_precision(route_weight, 8, 7)
    weight_low = route_weight - weight_high

    def selection(weight):
        return sum(
            jnp.where(slots[None, :] == slot_index[:, r, None], weight[:, r, None], 0.0)
            for r in range(ROUTES)
        ).astype(jnp.bfloat16)

    combine = jnp.concatenate([selection(weight_high), selection(weight_low)], 0)

    attn_rows = attend(query_rows, key_value_rows, sinks)

    expert_out = experts_call(expert_rows, wide_all)
    returned = exchange(expert_out, peer_count)
    both = jnp.dot(combine, returned, preferred_element_type=jnp.float32)
    total = both[:tokens_here] + both[tokens_here:]
    return (attn_rows, (resid_float + total).astype(jnp.bfloat16))


def solution(mesh):
    return jax.shard_map(
        per_device,
        mesh=mesh,
        in_specs=(
            P(("ctx", "exp"), None),
            P(("ctx", "exp"), None),
            P(("ctx", "exp"), None),
            P(("ctx", "exp"), None),
            P(),
            P(),
            P(("ctx", "exp")),
            P(("ctx", "exp"), None),
            P(("ctx", "exp"), None),
            P("exp", "ctx", None),
            P("exp", "ctx", None),
            P("exp", "ctx", None),
        ),
        out_specs=(P(("ctx", "exp"), None), P(("ctx", "exp"), None)),
        check_vma=False,
    )
```

```python
import math

import jax
import jax.numpy as jnp
from jax import lax
from jax.experimental import pallas as pl
from jax.experimental.pallas import tpu as pltpu
from jax.sharding import PartitionSpec as P

D = 1440
FFW = 1440
QHEADS = 32
KVHEADS = 4
HEAD = 64
WINDOW = 128
ROUTES = 2
CAP = 8
PANEL = 512
VMEM_BYTES = 60 * 1024 * 1024


def shifted(block, axis, distance):
    devices = range(lax.axis_size(axis))
    route = [(i - distance, i) for i in devices if i - distance in devices]
    return lax.ppermute(block, axis, route)


def pick_rows(choice, rows):
    return jnp.dot(choice, rows, preferred_element_type=jnp.float32).astype(jnp.bfloat16)


def panels(width):
    return [(low, min(low + PANEL, width)) for low in range(0, width, PANEL)]


def ring(block, forward_steps):
    count = lax.axis_size("ctx")
    behind, ahead = [block], [block]
    for step in range(max(forward_steps, count - 1 - forward_steps)):
        if step < forward_steps:
            route = [(i, (i + 1) % count) for i in range(count)]
            behind.append(lax.ppermute(behind[-1], "ctx", route))
        if step < count - 1 - forward_steps:
            route = [(i, (i - 1) % count) for i in range(count)]
            ahead.append(lax.ppermute(ahead[-1], "ctx", route))
    return [block] + behind[1:] + ahead[1:]


def ring_owner(forward_steps):
    count = lax.axis_size("ctx")
    shifts = [-step for step in range(forward_steps + 1)]
    shifts += [step for step in range(1, count - forward_steps)]
    return (lax.axis_index("ctx") + jnp.array(shifts, jnp.int32)) % count


def hidden_kernel(gate_owner, up_owner, rows_ref, *refs):
    out_ref, sliced, gate, upward, gate_sum, up_sum, hidden, arrival = refs[-8:]
    count = len(refs) // 2 - 4
    depth, width = gate.shape[1], gate.shape[2]
    copies = []
    for s in range(count):
        copies.append(pltpu.make_async_copy(refs[s], gate.at[s], arrival.at[0, s]))
        copies.append(pltpu.make_async_copy(refs[count + s], upward.at[s], arrival.at[1, s]))
    for copy in copies:
        copy.start()
    for s in range(count):
        sliced[s] = rows_ref[:, s * depth : (s + 1) * depth]
    for s in range(count):
        for side, owner, blocks, total in (
            (0, gate_owner, gate, gate_sum),
            (1, up_owner, upward, up_sum),
        ):
            copies[2 * s + side].wait()
            rows = sliced[owner[s]]
            for low, high in panels(width):
                part = jnp.dot(rows, blocks[s, :, low:high], preferred_element_type=jnp.float32)
                total[:, low:high] = part if s == 0 else total[:, low:high] + part
    for low, high in panels(width):
        hidden[:, low:high] = gated_hidden(gate_sum[:, low:high], up_sum[:, low:high])
    for s in range(count):
        out_ref[s] = hidden[:, s * depth : (s + 1) * depth]


def hidden_call(rows, gate_owner, up_owner, gate_blocks, up_blocks):
    count = len(gate_blocks)
    depth, width = gate_blocks[0].shape
    slots = rows.shape[0]
    whole = pl.BlockSpec(memory_space=pltpu.VMEM)
    scalars = pl.BlockSpec(memory_space=pltpu.SMEM)
    return pl.pallas_call(
        hidden_kernel,
        out_shape=jax.ShapeDtypeStruct((count, slots, depth), jnp.bfloat16),
        in_specs=[scalars, scalars, whole] + [pl.BlockSpec(memory_space=pltpu.HBM)] * (2 * count),
        out_specs=whole,
        scratch_shapes=[
            pltpu.VMEM((count, slots, depth), jnp.bfloat16),
            pltpu.VMEM((count, depth, width), jnp.bfloat16),
            pltpu.VMEM((count, depth, width), jnp.bfloat16),
            pltpu.VMEM((slots, width), jnp.float32),
            pltpu.VMEM((slots, width), jnp.float32),
            pltpu.VMEM((slots, width), jnp.bfloat16),
            pltpu.SemaphoreType.DMA((2, count)),
        ],
        compiler_params=pltpu.CompilerParams(vmem_limit_bytes=VMEM_BYTES),
        cost_estimate=pl.CostEstimate(
            flops=4 * slots * width * width,
            bytes_accessed=4 * width * width + 4 * slots * width,
            transcendentals=slots * width,
        ),
    )(gate_owner, up_owner, rows, *gate_blocks, *up_blocks)


def output_kernel(activ_ref, down_ref, out_ref, down, arrival):
    count = activ_ref.shape[0]
    copies = [
        pltpu.make_async_copy(down_ref.at[s], down.at[s], arrival.at[s]) for s in range(count)
    ]
    for copy in copies:
        copy.start()
    for low, high in panels(out_ref.shape[1]):
        total = jnp.zeros((out_ref.shape[0], high - low), jnp.float32)
        for s in range(count):
            if low == 0:
                copies[s].wait()
            total += jnp.dot(
                activ_ref[s], down[s, :, low:high], preferred_element_type=jnp.float32
            )
        out_ref[:, low:high] = total.astype(jnp.bfloat16)


def output_call(activ, down_all):
    count, slots, depth = activ.shape
    width = down_all.shape[2]
    whole = pl.BlockSpec(memory_space=pltpu.VMEM)
    return pl.pallas_call(
        output_kernel,
        out_shape=jax.ShapeDtypeStruct((slots, width), jnp.bfloat16),
        in_specs=[whole, pl.BlockSpec(memory_space=pltpu.HBM)],
        out_specs=whole,
        scratch_shapes=[
            pltpu.VMEM(down_all.shape, jnp.bfloat16),
            pltpu.SemaphoreType.DMA((count,)),
        ],
        compiler_params=pltpu.CompilerParams(vmem_limit_bytes=VMEM_BYTES),
        cost_estimate=pl.CostEstimate(
            flops=2 * slots * width * count * depth,
            bytes_accessed=2 * (width * count * depth + slots * count * depth + slots * width),
            transcendentals=0,
        ),
    )(activ, down_all)


def exchange(rows, peer_count):
    parts = rows.reshape(peer_count, -1, rows.shape[1])
    return lax.all_to_all(parts, "exp", split_axis=0, concat_axis=0, tiled=True).reshape(rows.shape)


def gated_hidden(gate, upward):
    return (gate * jax.nn.sigmoid(1.702 * gate) * (upward + 1.0)).astype(jnp.bfloat16)


def attend(query_rows, key_value_rows, sinks):
    tokens_here = query_rows.shape[0]
    previous = shifted(key_value_rows, ("ctx", "exp"), 1)
    span_rows = WINDOW + tokens_here
    groups = QHEADS // KVHEADS
    span = jnp.concatenate([previous, key_value_rows], 0)
    all_keys = span[:, : KVHEADS * HEAD].reshape(span_rows, KVHEADS, HEAD)
    all_values = span[:, KVHEADS * HEAD :].reshape(span_rows, KVHEADS, HEAD)
    query_heads = query_rows.reshape(tokens_here, KVHEADS, groups, HEAD)
    scores = jnp.einsum(
        "ihgd,jhd->hgij", query_heads, all_keys, preferred_element_type=jnp.float32
    ) * (1.0 / math.sqrt(HEAD))
    first_row = lax.axis_index(("ctx", "exp")) * tokens_here
    query_place = first_row + jnp.arange(tokens_here, dtype=jnp.int32)
    key_place = first_row - WINDOW + jnp.arange(span_rows, dtype=jnp.int32)
    distance = query_place[:, None] - key_place[None, :]
    allowed = (distance >= 0) & (distance < WINDOW) & (key_place >= 0)[None, :]
    scores = jnp.where(allowed, scores, -1e30)
    sink_logit = sinks.reshape(KVHEADS, groups)[:, :, None]
    row_max = jnp.maximum(jnp.max(scores, -1), sink_logit)
    expo_terms = jnp.exp(scores - row_max[..., None])
    denom_total = jnp.sum(expo_terms, -1) + jnp.exp(sink_logit - row_max)
    probs = (expo_terms / denom_total[..., None]).astype(jnp.bfloat16)
    attended = jnp.einsum("hgij,jhd->ihgd", probs, all_values, preferred_element_type=jnp.float32)
    return attended.reshape(tokens_here, QHEADS * HEAD).astype(jnp.bfloat16)


def per_device(
    hidden_rows,
    queries,
    keys,
    values,
    sinks,
    norm_gain,
    learner_row,
    expert_ids,
    route_weight,
    gate_w,
    up_w,
    down_w,
):
    tokens_here = hidden_rows.shape[0]
    peer_count = lax.axis_size("exp")
    per_peer = tokens_here // peer_count
    gate_block, up_block, down_block = gate_w[0], up_w[0], down_w[0]

    count = lax.axis_size("ctx")
    forward = {"gate": count // 2, "up": count - 1 - count // 2}
    blocks = {"gate": ring(gate_block, forward["gate"]), "up": ring(up_block, forward["up"])}

    def after_steps(value, **steps):
        held = []
        for name, step in steps.items():
            places = [step] if step <= forward[name] else []
            places += [forward[name] + step] if forward[name] + step < count else []
            held += [(name, place) for place in places]
        barred = lax.optimization_barrier((value, [blocks[name][place] for name, place in held]))
        for (name, place), block in zip(held, barred[1]):
            blocks[name][place] = block
        return barred[0]

    slot = learner_row % (peer_count * tokens_here) // tokens_here * per_peer + learner_row % per_peer
    order = (jnp.arange(tokens_here, dtype=jnp.int32)[:, None] == slot[None, :]).astype(jnp.bfloat16)
    packed = jnp.concatenate([queries, keys, values, hidden_rows], 1)
    arrived = exchange(pick_rows(order, packed), peer_count)
    arrived = after_steps(arrived, gate=1, up=1)
    arrived, down_block = lax.optimization_barrier((arrived, down_block))
    down_all = lax.all_gather(down_block, "ctx", axis=0)
    query_rows = arrived[:, : QHEADS * HEAD]
    key_value_rows = arrived[:, QHEADS * HEAD : (QHEADS + 2 * KVHEADS) * HEAD]
    resid = arrived[:, (QHEADS + 2 * KVHEADS) * HEAD :]
    resid_float = resid.astype(jnp.float32)
    mean_square = jnp.mean(resid_float * resid_float, -1, keepdims=True)
    normed = (resid_float * lax.rsqrt(mean_square + 1e-05) * norm_gain).astype(jnp.bfloat16)

    slots_total = peer_count * CAP
    pair_count = tokens_here * ROUTES
    pair_expert = expert_ids.reshape(-1)
    hits = pair_expert[:, None] == jnp.arange(peer_count, dtype=jnp.int32)[None, :]
    pair_place = jnp.arange(pair_count, dtype=jnp.int32)
    before = (pair_place[:, None] > pair_place[None, :]).astype(jnp.bfloat16)
    earlier = jnp.dot(before, hits.astype(jnp.bfloat16), preferred_element_type=jnp.float32)
    pair_rank = jnp.sum(jnp.where(hits, earlier, 0.0), 1).astype(jnp.int32)
    slot_index = (pair_expert * CAP + pair_rank).reshape(tokens_here, ROUTES)
    slots = jnp.arange(slots_total, dtype=jnp.int32)
    sent = sum(slots[:, None] == slot_index[None, :, r] for r in range(ROUTES))
    outgoing = pick_rows(sent.astype(jnp.bfloat16), normed)
    outgoing = after_steps(outgoing, gate=2)
    expert_rows = exchange(outgoing, peer_count)
    weight_high = lax.reduce_precision(route_weight, 8, 7)
    weight_low = route_weight - weight_high

    def selection(weight):
        return sum(
            jnp.where(slots[None, :] == slot_index[:, r, None], weight[:, r, None], 0.0)
            for r in range(ROUTES)
        ).astype(jnp.bfloat16)

    combine = jnp.concatenate([selection(weight_high), selection(weight_low)], 0)

    attn_rows = attend(query_rows, key_value_rows, sinks)

    activ = hidden_call(
        expert_rows,
        ring_owner(forward["gate"]),
        ring_owner(forward["up"]),
        blocks["gate"],
        blocks["up"],
    )
    expert_out = output_call(activ, down_all)
    returned = exchange(expert_out, peer_count)
    both = jnp.dot(combine, returned, preferred_element_type=jnp.float32)
    total = both[:tokens_here] + both[tokens_here:]
    return (attn_rows, (resid_float + total).astype(jnp.bfloat16))


def solution(mesh):
    return jax.shard_map(
        per_device,
        mesh=mesh,
        in_specs=(
            P(("ctx", "exp"), None),
            P(("ctx", "exp"), None),
            P(("ctx", "exp"), None),
            P(("ctx", "exp"), None),
            P(),
            P(),
            P(("ctx", "exp")),
            P(("ctx", "exp"), None),
            P(("ctx", "exp"), None),
            P("exp", "ctx", None),
            P("exp", "ctx", None),
            P("exp", "ctx", None),
        ),
        out_specs=(P(("ctx", "exp"), None), P(("ctx", "exp"), None)),
        check_vma=False,
    )
```

```python
import math

import jax
import jax.numpy as jnp
from jax import lax
from jax.experimental import pallas as pl
from jax.experimental.pallas import tpu as pltpu
from jax.sharding import PartitionSpec as P

D = 1440
FFW = 1440
QHEADS = 32
KVHEADS = 4
HEAD = 64
WINDOW = 128
ROUTES = 2
CAP = 8
LANES = 128
PANEL = 512
FIRST = 960
VMEM_BYTES = 60 * 1024 * 1024


def shifted(block, axis, distance):
    devices = range(lax.axis_size(axis))
    route = [(i - distance, i) for i in devices if i - distance in devices]
    return lax.ppermute(block, axis, route)


def pick_rows(choice, rows):
    return jnp.dot(choice, rows, preferred_element_type=jnp.float32).astype(jnp.bfloat16)


def panels(width):
    return [(low, min(low + PANEL, width)) for low in range(0, width, PANEL)]


def pack_kernel(gate_ref, up_ref, down_ref, first_ref, second_ref):
    width = gate_ref.shape[1]
    first_ref[:, :width] = gate_ref[...]
    first_ref[:, width : 2 * width] = up_ref[...]
    first_ref[:, 2 * width :] = down_ref[:, :FIRST]
    second_ref[...] = down_ref[:, FIRST:]


def pack_call(gate_block, up_block, down_block):
    depth, width = gate_block.shape
    shapes = [(depth, 2 * width + FIRST), (depth, width - FIRST)]
    return pl.pallas_call(
        pack_kernel,
        out_shape=[jax.ShapeDtypeStruct(shape, jnp.bfloat16) for shape in shapes],
        cost_estimate=pl.CostEstimate(
            flops=0, bytes_accessed=12 * depth * width, transcendentals=0
        ),
    )(gate_block, up_block, down_block)


def project_down(sliced, weights, start, width, total, out_ref):
    count = sliced.shape[0]
    base = start // LANES * LANES
    for low, high in panels(start + width - base):
        part = jnp.zeros((out_ref.shape[0], high - low), jnp.float32)
        for s in range(count):
            part += jnp.dot(
                sliced[s], weights[s, :, base + low : base + high], preferred_element_type=jnp.float32
            )
        total[:, low:high] = part
    out_ref[...] = total[:, start - base : start - base + width].astype(jnp.bfloat16)


def first_kernel(rows_ref, wide_ref, out_ref, activ_ref, sliced, wide, total, hidden, arrival):
    count, depth, packed = wide_ref.shape
    width = rows_ref.shape[1]
    cuts = panels(total.shape[1])
    pieces = cuts + [(total.shape[1], packed)]
    copies = []
    for place, (low, high) in enumerate(pieces):
        piece = (slice(None), slice(None), pl.ds(low, high - low))
        copies.append(
            pltpu.make_async_copy(wide_ref.at[piece], wide.at[piece], arrival.at[place])
        )
        copies[-1].start()
    for s in range(count):
        sliced[s] = rows_ref[:, s * depth : (s + 1) * depth]
    for place, (low, high) in enumerate(cuts):
        copies[place].wait()
        part = jnp.zeros((rows_ref.shape[0], high - low), jnp.float32)
        for s in range(count):
            part += jnp.dot(sliced[s], wide[s, :, low:high], preferred_element_type=jnp.float32)
        total[:, low:high] = part
    for low, high in panels(width):
        hidden[:, low:high] = gated_hidden(
            total[:, low:high], total[:, width + low : width + high]
        )
    for s in range(count):
        activ_ref[s] = hidden[:, s * depth : (s + 1) * depth]
    copies[-1].wait()
    project_down(activ_ref, wide, 2 * width, packed - 2 * width, total, out_ref)


def first_call(rows, wide_all):
    count, depth, packed = wide_all.shape
    slots, width = rows.shape
    whole = pl.BlockSpec(memory_space=pltpu.VMEM)
    summed = -(-2 * width // LANES) * LANES
    return pl.pallas_call(
        first_kernel,
        out_shape=[
            jax.ShapeDtypeStruct((slots, packed - 2 * width), jnp.bfloat16),
            jax.ShapeDtypeStruct((count, slots, depth), jnp.bfloat16),
        ],
        in_specs=[whole, pl.BlockSpec(memory_space=pltpu.HBM)],
        out_specs=[whole, whole],
        scratch_shapes=[
            pltpu.VMEM((count, slots, depth), jnp.bfloat16),
            pltpu.VMEM(wide_all.shape, jnp.bfloat16),
            pltpu.VMEM((slots, summed), jnp.float32),
            pltpu.VMEM((slots, width), jnp.bfloat16),
            pltpu.SemaphoreType.DMA((len(panels(summed)) + 1,)),
        ],
        compiler_params=pltpu.CompilerParams(vmem_limit_bytes=VMEM_BYTES),
        cost_estimate=pl.CostEstimate(
            flops=2 * slots * width * packed,
            bytes_accessed=2 * count * depth * packed + 4 * slots * width,
            transcendentals=slots * width,
        ),
    )(rows, wide_all)


def second_kernel(activ_ref, rest_ref, out_ref, total):
    project_down(activ_ref, rest_ref, 0, out_ref.shape[1], total, out_ref)


def second_call(activ, rest_all):
    count, slots, depth = activ.shape
    width = rest_all.shape[2]
    whole = pl.BlockSpec(memory_space=pltpu.VMEM)
    return pl.pallas_call(
        second_kernel,
        out_shape=jax.ShapeDtypeStruct((slots, width), jnp.bfloat16),
        in_specs=[whole, whole],
        out_specs=whole,
        scratch_shapes=[pltpu.VMEM((slots, width), jnp.float32)],
        compiler_params=pltpu.CompilerParams(vmem_limit_bytes=VMEM_BYTES),
        cost_estimate=pl.CostEstimate(
            flops=2 * slots * width * count * depth,
            bytes_accessed=2 * (count * depth * (slots + width) + slots * width),
            transcendentals=0,
        ),
    )(activ, rest_all)


def exchange(rows, peer_count):
    parts = rows.reshape(peer_count, -1, rows.shape[1])
    return lax.all_to_all(parts, "exp", split_axis=0, concat_axis=0, tiled=True).reshape(rows.shape)


def gated_hidden(gate, upward):
    return (gate * jax.nn.sigmoid(1.702 * gate) * (upward + 1.0)).astype(jnp.bfloat16)


def attend(query_rows, key_value_rows, sinks):
    tokens_here = query_rows.shape[0]
    previous = shifted(key_value_rows, ("ctx", "exp"), 1)
    span_rows = WINDOW + tokens_here
    groups = QHEADS // KVHEADS
    span = jnp.concatenate([previous, key_value_rows], 0)
    all_keys = span[:, : KVHEADS * HEAD].reshape(span_rows, KVHEADS, HEAD)
    all_values = span[:, KVHEADS * HEAD :].reshape(span_rows, KVHEADS, HEAD)
    query_heads = query_rows.reshape(tokens_here, KVHEADS, groups, HEAD)
    scores = jnp.einsum(
        "ihgd,jhd->hgij", query_heads, all_keys, preferred_element_type=jnp.float32
    ) * (1.0 / math.sqrt(HEAD))
    first_row = lax.axis_index(("ctx", "exp")) * tokens_here
    query_place = first_row + jnp.arange(tokens_here, dtype=jnp.int32)
    key_place = first_row - WINDOW + jnp.arange(span_rows, dtype=jnp.int32)
    distance = query_place[:, None] - key_place[None, :]
    allowed = (distance >= 0) & (distance < WINDOW) & (key_place >= 0)[None, :]
    scores = jnp.where(allowed, scores, -1e30)
    sink_logit = sinks.reshape(KVHEADS, groups)[:, :, None]
    row_max = jnp.maximum(jnp.max(scores, -1), sink_logit)
    expo_terms = jnp.exp(scores - row_max[..., None])
    denom_total = jnp.sum(expo_terms, -1) + jnp.exp(sink_logit - row_max)
    probs = (expo_terms / denom_total[..., None]).astype(jnp.bfloat16)
    attended = jnp.einsum("hgij,jhd->ihgd", probs, all_values, preferred_element_type=jnp.float32)
    return attended.reshape(tokens_here, QHEADS * HEAD).astype(jnp.bfloat16)


def per_device(
    hidden_rows,
    queries,
    keys,
    values,
    sinks,
    norm_gain,
    learner_row,
    expert_ids,
    route_weight,
    gate_w,
    up_w,
    down_w,
):
    tokens_here = hidden_rows.shape[0]
    peer_count = lax.axis_size("exp")
    per_peer = tokens_here // peer_count
    gate_block, up_block, down_block = gate_w[0], up_w[0], down_w[0]

    wide, rest = pack_call(gate_block, up_block, down_block)
    wide_all = lax.all_gather(wide, "ctx", axis=0)

    slot = learner_row % (peer_count * tokens_here) // tokens_here * per_peer + learner_row % per_peer
    order = (jnp.arange(tokens_here, dtype=jnp.int32)[:, None] == slot[None, :]).astype(jnp.bfloat16)
    resid = exchange(pick_rows(order, hidden_rows), peer_count)
    resid_float = resid.astype(jnp.float32)
    mean_square = jnp.mean(resid_float * resid_float, -1, keepdims=True)
    normed = (resid_float * lax.rsqrt(mean_square + 1e-05) * norm_gain).astype(jnp.bfloat16)

    slots_total = peer_count * CAP
    pair_count = tokens_here * ROUTES
    pair_expert = expert_ids.reshape(-1)
    hits = pair_expert[:, None] == jnp.arange(peer_count, dtype=jnp.int32)[None, :]
    pair_place = jnp.arange(pair_count, dtype=jnp.int32)
    before = (pair_place[:, None] > pair_place[None, :]).astype(jnp.bfloat16)
    earlier = jnp.dot(before, hits.astype(jnp.bfloat16), preferred_element_type=jnp.float32)
    pair_rank = jnp.sum(jnp.where(hits, earlier, 0.0), 1).astype(jnp.int32)
    slot_index = (pair_expert * CAP + pair_rank).reshape(tokens_here, ROUTES)
    slots = jnp.arange(slots_total, dtype=jnp.int32)
    sent = sum(slots[:, None] == slot_index[None, :, r] for r in range(ROUTES))
    outgoing = pick_rows(sent.astype(jnp.bfloat16), normed)
    expert_rows = exchange(outgoing, peer_count)
    packed = jnp.concatenate([queries, keys, values], 1)
    expert_rows, packed = lax.optimization_barrier((expert_rows, packed))
    arrived = exchange(pick_rows(order, packed), peer_count)
    query_rows = arrived[:, : QHEADS * HEAD]
    key_value_rows = arrived[:, QHEADS * HEAD :]
    weight_high = lax.reduce_precision(route_weight, 8, 7)
    weight_low = route_weight - weight_high

    def selection(weight):
        return sum(
            jnp.where(slots[None, :] == slot_index[:, r, None], weight[:, r, None], 0.0)
            for r in range(ROUTES)
        ).astype(jnp.bfloat16)

    combine = jnp.concatenate([selection(weight_high), selection(weight_low)], 0)

    attn_rows = attend(query_rows, key_value_rows, sinks)

    wide_all, rest = lax.optimization_barrier((wide_all, rest))
    rest_all = lax.all_gather(rest, "ctx", axis=0)
    first_out, activ = first_call(expert_rows, wide_all)

    def combined(expert_out, low):
        returned = exchange(expert_out, peer_count)
        both = jnp.dot(combine, returned, preferred_element_type=jnp.float32)
        total = both[:tokens_here] + both[tokens_here:]
        return (resid_float[:, low : low + total.shape[1]] + total).astype(jnp.bfloat16)

    mixed = [combined(first_out, 0), combined(second_call(activ, rest_all), FIRST)]
    return (attn_rows, jnp.concatenate(mixed, 1))


def solution(mesh):
    return jax.shard_map(
        per_device,
        mesh=mesh,
        in_specs=(
            P(("ctx", "exp"), None),
            P(("ctx", "exp"), None),
            P(("ctx", "exp"), None),
            P(("ctx", "exp"), None),
            P(),
            P(),
            P(("ctx", "exp")),
            P(("ctx", "exp"), None),
            P(("ctx", "exp"), None),
            P("exp", "ctx", None),
            P("exp", "ctx", None),
            P("exp", "ctx", None),
        ),
        out_specs=(P(("ctx", "exp"), None), P(("ctx", "exp"), None)),
        check_vma=False,
    )
```

```python
import math

import jax
import jax.numpy as jnp
from jax import lax
from jax.experimental import pallas as pl
from jax.experimental.pallas import tpu as pltpu
from jax.sharding import PartitionSpec as P

D = 1440
FFW = 1440
QHEADS = 32
KVHEADS = 4
HEAD = 64
WINDOW = 128
ROUTES = 2
CAP = 8
LANES = 128
WIDE = 256
GROUPS = ((0, 4), (4, 8), (8, 11))
VMEM_BYTES = 60 * 1024 * 1024


def shifted(block, axis, distance):
    devices = range(lax.axis_size(axis))
    route = [(i - distance, i) for i in devices if i - distance in devices]
    return lax.ppermute(block, axis, route)


def pick_rows(choice, rows):
    return jnp.dot(choice, rows, preferred_element_type=jnp.float32).astype(jnp.bfloat16)


def pack_kernel(gate_ref, up_ref, down_ref, packed_ref):
    depth, width = gate_ref.shape
    main = width // LANES * LANES
    left = width - main
    for place, ref in enumerate((gate_ref, up_ref, down_ref)):
        packed_ref[:, place * main : (place + 1) * main] = ref[:, :main]
        start = 3 * main + place * left
        packed_ref[:, start : start + left] = ref[:, main:]
    packed_ref[:, 3 * width :] = jnp.zeros((depth, packed_ref.shape[1] - 3 * width), jnp.bfloat16)


def pack_call(gate_block, up_block, down_block):
    depth, width = gate_block.shape
    packed = 3 * (width // LANES) * LANES + LANES
    return pl.pallas_call(
        pack_kernel,
        out_shape=jax.ShapeDtypeStruct((depth, packed), jnp.bfloat16),
        cost_estimate=pl.CostEstimate(
            flops=0, bytes_accessed=12 * depth * width, transcendentals=0
        ),
    )(gate_block, up_block, down_block)


def slice_kernel(rows_ref, sliced_ref):
    count, _, depth = sliced_ref.shape
    for s in range(count):
        sliced_ref[s] = rows_ref[:, s * depth : (s + 1) * depth]


def slice_call(rows, count):
    slots, width = rows.shape
    return pl.pallas_call(
        slice_kernel,
        out_shape=jax.ShapeDtypeStruct((count, slots, width // count), jnp.bfloat16),
        cost_estimate=pl.CostEstimate(
            flops=0, bytes_accessed=4 * slots * width, transcendentals=0
        ),
    )(rows)


def experts_kernel(sliced_ref, wide_ref, out_ref, wide, hidden, resliced, arrival):
    count, depth, packed = wide_ref.shape
    slots, width = out_ref.shape
    main = width // LANES * LANES
    left = width - main
    pieces = []
    for low, high in GROUPS:
        pieces.append((low * LANES, high * LANES))
        pieces.append((main + low * LANES, main + high * LANES))
    pieces.append((2 * main, packed))
    copies = []
    for place, (low, high) in enumerate(pieces):
        piece = (slice(None), slice(None), pl.ds(low, high - low))
        copies.append(
            pltpu.make_async_copy(wide_ref.at[piece], wide.at[piece], arrival.at[place])
        )
        copies[-1].start()

    def summed(left_ref, columns):
        total = jnp.zeros((slots, WIDE), jnp.float32)
        for s in range(count):
            total += jnp.dot(left_ref[s], columns(s), preferred_element_type=jnp.float32)
        return total

    def hidden_tile(tile, carry):
        low = pl.multiple_of(tile * LANES, LANES)
        high = pl.multiple_of(main + tile * LANES, LANES)
        both = summed(
            sliced_ref,
            lambda s: jnp.concatenate(
                [wide[s, :, pl.ds(low, LANES)], wide[s, :, pl.ds(high, LANES)]], 1
            ),
        )
        hidden[:, pl.ds(low, LANES)] = gated_hidden(both[:, :LANES], both[:, LANES:])
        return carry

    for group, (low, high) in enumerate(GROUPS):
        copies[2 * group].wait()
        copies[2 * group + 1].wait()
        lax.fori_loop(low, high, hidden_tile, 0)
    copies[-1].wait()
    rest = summed(sliced_ref, lambda s: wide[s, :, packed - WIDE :])[:, LANES:]
    hidden[:, main:] = gated_hidden(rest[:, :left], rest[:, left : 2 * left])
    for s in range(count):
        resliced[s] = hidden[:, s * depth : (s + 1) * depth]

    def output_tiles(place, carry):
        low = pl.multiple_of(place * WIDE, WIDE)
        source = pl.multiple_of(2 * main + place * WIDE, LANES)
        total = summed(resliced, lambda s: wide[s, :, pl.ds(source, WIDE)])
        out_ref[:, pl.ds(low, WIDE)] = total.astype(jnp.bfloat16)
        return carry

    whole = main // WIDE
    lax.fori_loop(0, whole, output_tiles, 0)
    last = summed(resliced, lambda s: wide[s, :, packed - WIDE :]).astype(jnp.bfloat16)
    out_ref[:, whole * WIDE : main] = last[:, :LANES]
    out_ref[:, main:] = last[:, LANES + 2 * left : LANES + 3 * left]


def experts_call(sliced, wide_all):
    count, slots, depth = sliced.shape
    width = count * depth
    whole = pl.BlockSpec(memory_space=pltpu.VMEM)
    return pl.pallas_call(
        experts_kernel,
        out_shape=jax.ShapeDtypeStruct((slots, width), jnp.bfloat16),
        in_specs=[whole, pl.BlockSpec(memory_space=pltpu.HBM)],
        out_specs=whole,
        scratch_shapes=[
            pltpu.VMEM(wide_all.shape, jnp.bfloat16),
            pltpu.VMEM((slots, width), jnp.bfloat16),
            pltpu.VMEM((count, slots, depth), jnp.bfloat16),
            pltpu.SemaphoreType.DMA((2 * len(GROUPS) + 1,)),
        ],
        compiler_params=pltpu.CompilerParams(vmem_limit_bytes=VMEM_BYTES),
        cost_estimate=pl.CostEstimate(
            flops=6 * slots * width * width,
            bytes_accessed=6 * width * width + 4 * slots * width,
            transcendentals=slots * width,
        ),
    )(sliced, wide_all)


def exchange(rows, peer_count):
    parts = rows.reshape(peer_count, -1, rows.shape[1])
    return lax.all_to_all(parts, "exp", split_axis=0, concat_axis=0, tiled=True).reshape(rows.shape)


def gated_hidden(gate, upward):
    return (gate * jax.nn.sigmoid(1.702 * gate) * (upward + 1.0)).astype(jnp.bfloat16)


def attend(query_rows, key_value_rows, sinks):
    tokens_here = query_rows.shape[0]
    previous = shifted(key_value_rows, ("ctx", "exp"), 1)
    span_rows = WINDOW + tokens_here
    groups = QHEADS // KVHEADS
    span = jnp.concatenate([previous, key_value_rows], 0)
    all_keys = span[:, : KVHEADS * HEAD].reshape(span_rows, KVHEADS, HEAD)
    all_values = span[:, KVHEADS * HEAD :].reshape(span_rows, KVHEADS, HEAD)
    query_heads = query_rows.reshape(tokens_here, KVHEADS, groups, HEAD)
    scores = jnp.einsum(
        "ihgd,jhd->hgij", query_heads, all_keys, preferred_element_type=jnp.float32
    ) * (1.0 / math.sqrt(HEAD))
    first_row = lax.axis_index(("ctx", "exp")) * tokens_here
    query_place = first_row + jnp.arange(tokens_here, dtype=jnp.int32)
    key_place = first_row - WINDOW + jnp.arange(span_rows, dtype=jnp.int32)
    distance = query_place[:, None] - key_place[None, :]
    allowed = (distance >= 0) & (distance < WINDOW) & (key_place >= 0)[None, :]
    scores = jnp.where(allowed, scores, -1e30)
    sink_logit = sinks.reshape(KVHEADS, groups)[:, :, None]
    row_max = jnp.maximum(jnp.max(scores, -1), sink_logit)
    expo_terms = jnp.exp(scores - row_max[..., None])
    denom_total = jnp.sum(expo_terms, -1) + jnp.exp(sink_logit - row_max)
    probs = (expo_terms / denom_total[..., None]).astype(jnp.bfloat16)
    attended = jnp.einsum("hgij,jhd->ihgd", probs, all_values, preferred_element_type=jnp.float32)
    return attended.reshape(tokens_here, QHEADS * HEAD).astype(jnp.bfloat16)


def per_device(
    hidden_rows,
    queries,
    keys,
    values,
    sinks,
    norm_gain,
    learner_row,
    expert_ids,
    route_weight,
    gate_w,
    up_w,
    down_w,
):
    tokens_here = hidden_rows.shape[0]
    peer_count = lax.axis_size("exp")
    per_peer = tokens_here // peer_count
    gate_block, up_block, down_block = gate_w[0], up_w[0], down_w[0]

    wide_all = lax.all_gather(pack_call(gate_block, up_block, down_block), "ctx", axis=0)

    slot = learner_row % (peer_count * tokens_here) // tokens_here * per_peer + learner_row % per_peer
    order = (jnp.arange(tokens_here, dtype=jnp.int32)[:, None] == slot[None, :]).astype(jnp.bfloat16)
    resid = exchange(pick_rows(order, hidden_rows), peer_count)
    resid_float = resid.astype(jnp.float32)
    mean_square = jnp.mean(resid_float * resid_float, -1, keepdims=True)
    normed = (resid_float * lax.rsqrt(mean_square + 1e-05) * norm_gain).astype(jnp.bfloat16)

    slots_total = peer_count * CAP
    pair_count = tokens_here * ROUTES
    pair_expert = expert_ids.reshape(-1)
    hits = pair_expert[:, None] == jnp.arange(peer_count, dtype=jnp.int32)[None, :]
    pair_place = jnp.arange(pair_count, dtype=jnp.int32)
    before = (pair_place[:, None] > pair_place[None, :]).astype(jnp.bfloat16)
    earlier = jnp.dot(before, hits.astype(jnp.bfloat16), preferred_element_type=jnp.float32)
    pair_rank = jnp.sum(jnp.where(hits, earlier, 0.0), 1).astype(jnp.int32)
    slot_index = (pair_expert * CAP + pair_rank).reshape(tokens_here, ROUTES)
    slots = jnp.arange(slots_total, dtype=jnp.int32)
    sent = sum(slots[:, None] == slot_index[None, :, r] for r in range(ROUTES))
    outgoing = pick_rows(sent.astype(jnp.bfloat16), normed)
    expert_rows = exchange(outgoing, peer_count)
    packed = jnp.concatenate([queries, keys, values], 1)
    expert_rows, packed = lax.optimization_barrier((expert_rows, packed))
    sliced = slice_call(expert_rows, lax.axis_size("ctx"))
    arrived = exchange(pick_rows(order, packed), peer_count)
    query_rows = arrived[:, : QHEADS * HEAD]
    key_value_rows = arrived[:, QHEADS * HEAD :]
    weight_high = lax.reduce_precision(route_weight, 8, 7)
    weight_low = route_weight - weight_high

    def selection(weight):
        return sum(
            jnp.where(slots[None, :] == slot_index[:, r, None], weight[:, r, None], 0.0)
            for r in range(ROUTES)
        ).astype(jnp.bfloat16)

    combine = jnp.concatenate([selection(weight_high), selection(weight_low)], 0)

    attn_rows = attend(query_rows, key_value_rows, sinks)

    expert_out = experts_call(sliced, wide_all)
    returned = exchange(expert_out, peer_count)
    both = jnp.dot(combine, returned, preferred_element_type=jnp.float32)
    total = both[:tokens_here] + both[tokens_here:]
    return (attn_rows, (resid_float + total).astype(jnp.bfloat16))


def solution(mesh):
    return jax.shard_map(
        per_device,
        mesh=mesh,
        in_specs=(
            P(("ctx", "exp"), None),
            P(("ctx", "exp"), None),
            P(("ctx", "exp"), None),
            P(("ctx", "exp"), None),
            P(),
            P(),
            P(("ctx", "exp")),
            P(("ctx", "exp"), None),
            P(("ctx", "exp"), None),
            P("exp", "ctx", None),
            P("exp", "ctx", None),
            P("exp", "ctx", None),
        ),
        out_specs=(P(("ctx", "exp"), None), P(("ctx", "exp"), None)),
        check_vma=False,
    )
```

```python
import math

import jax
import jax.numpy as jnp
from jax import lax
from jax.experimental import pallas as pl
from jax.experimental.pallas import tpu as pltpu
from jax.sharding import PartitionSpec as P

D = 1440
FFW = 1440
QHEADS = 32
KVHEADS = 4
HEAD = 64
WINDOW = 128
ROUTES = 2
CAP = 8
LANES = 128
ROWS = 8
GROUPS = ((0, 2), (2, 4), (4, 5))
VMEM_BYTES = 60 * 1024 * 1024


def shifted(block, axis, distance):
    devices = range(lax.axis_size(axis))
    route = [(i - distance, i) for i in devices if i - distance in devices]
    return lax.ppermute(block, axis, route)


def pick_rows(choice, rows):
    return jnp.dot(choice, rows, preferred_element_type=jnp.float32).astype(jnp.bfloat16)


def pitch_of(depth):
    return -(-depth // ROWS) * ROWS


def pack_kernel(gate_ref, up_ref, down_ref, packed_ref):
    depth, width = gate_ref.shape
    main = width // LANES * LANES
    left = width - main
    pitch, packed = packed_ref.shape
    packed_ref[depth:, :] = jnp.zeros((pitch - depth, packed), jnp.bfloat16)
    for place, ref in enumerate((gate_ref, up_ref, down_ref)):
        packed_ref[:depth, place * main : (place + 1) * main] = ref[:, :main]
        start = 3 * main + place * left
        packed_ref[:depth, start : start + left] = ref[:, main:]
    packed_ref[:depth, 3 * width :] = jnp.zeros((depth, packed - 3 * width), jnp.bfloat16)


def pack_call(gate_block, up_block, down_block):
    depth, width = gate_block.shape
    packed = 3 * (width // LANES) * LANES + LANES
    return pl.pallas_call(
        pack_kernel,
        out_shape=jax.ShapeDtypeStruct((pitch_of(depth), packed), jnp.bfloat16),
        cost_estimate=pl.CostEstimate(
            flops=0, bytes_accessed=12 * depth * width, transcendentals=0
        ),
    )(gate_block, up_block, down_block)


def spread(source, target, depth):
    pitch = pitch_of(depth)
    for s in range(source.shape[1] // depth):
        target[:, s * pitch : s * pitch + depth] = source[:, s * depth : (s + 1) * depth]
        target[:, s * pitch + depth : (s + 1) * pitch] = jnp.zeros(
            (source.shape[0], pitch - depth), jnp.bfloat16
        )


def spread_call(rows, depth):
    slots, width = rows.shape

    def spread_kernel(rows_ref, spread_ref):
        spread(rows_ref, spread_ref, depth)

    return pl.pallas_call(
        spread_kernel,
        out_shape=jax.ShapeDtypeStruct((slots, width // depth * pitch_of(depth)), jnp.bfloat16),
        cost_estimate=pl.CostEstimate(
            flops=0, bytes_accessed=4 * slots * width, transcendentals=0
        ),
    )(rows)


def experts_kernel(depth, rows_ref, wide_ref, out_ref, wide, hidden, again, arrival):
    packed = wide_ref.shape[1]
    width = out_ref.shape[1]
    main = width // LANES * LANES
    left = width - main
    step = 2 * LANES
    pieces = []
    for low, high in GROUPS:
        pieces.append((low * step, high * step))
        pieces.append((main + low * step, main + high * step))
    done = GROUPS[-1][1] * step
    pieces += [(done, main), (main + done, packed)]
    copies = []
    for place, (low, high) in enumerate(pieces):
        piece = (slice(None), pl.ds(low, high - low))
        copies.append(
            pltpu.make_async_copy(wide_ref.at[piece], wide.at[piece], arrival.at[place])
        )
        copies[-1].start()

    def product(left_ref, columns):
        return jnp.dot(left_ref[...], columns, preferred_element_type=jnp.float32)

    def hidden_tiles(place, carry):
        low = pl.multiple_of(place * step, step)
        high = pl.multiple_of(main + place * step, LANES)
        both = product(
            rows_ref, jnp.concatenate([wide[:, pl.ds(low, step)], wide[:, pl.ds(high, step)]], 1)
        )
        hidden[:, pl.ds(low, step)] = gated_hidden(both[:, :step], both[:, step:])
        return carry

    for group, (low, high) in enumerate(GROUPS):
        copies[2 * group].wait()
        copies[2 * group + 1].wait()
        lax.fori_loop(low, high, hidden_tiles, 0)
    copies[-2].wait()
    copies[-1].wait()
    both = product(
        rows_ref,
        jnp.concatenate(
            [wide[:, done:main], wide[:, main + done : 2 * main], wide[:, 3 * main :]], 1
        ),
    )
    span = main - done
    rest = both[:, 2 * span :]
    hidden[:, done:main] = gated_hidden(both[:, :span], both[:, span : 2 * span])
    hidden[:, main:] = gated_hidden(rest[:, :left], rest[:, left : 2 * left])
    spread(hidden, again, depth)

    def output_tiles(place, carry):
        low = pl.multiple_of(place * 2 * step, 2 * step)
        source = pl.multiple_of(2 * main + place * 2 * step, LANES)
        total = product(again, wide[:, pl.ds(source, 2 * step)])
        out_ref[:, pl.ds(low, 2 * step)] = total.astype(jnp.bfloat16)
        return carry

    whole = main // (2 * step)
    lax.fori_loop(0, whole, output_tiles, 0)
    first = whole * 2 * step
    last = product(again, wide[:, 2 * main + first :]).astype(jnp.bfloat16)
    out_ref[:, first:main] = last[:, : main - first]
    tail = main - first + 2 * left
    out_ref[:, main:] = last[:, tail : tail + left]


def experts_call(rows, wide_all, depth, width):
    slots = rows.shape[0]
    whole = pl.BlockSpec(memory_space=pltpu.VMEM)

    def kernel(*refs):
        experts_kernel(depth, *refs)

    return pl.pallas_call(
        kernel,
        out_shape=jax.ShapeDtypeStruct((slots, width), jnp.bfloat16),
        in_specs=[whole, pl.BlockSpec(memory_space=pltpu.HBM)],
        out_specs=whole,
        scratch_shapes=[
            pltpu.VMEM(wide_all.shape, jnp.bfloat16),
            pltpu.VMEM((slots, width), jnp.bfloat16),
            pltpu.VMEM(rows.shape, jnp.bfloat16),
            pltpu.SemaphoreType.DMA((2 * len(GROUPS) + 2,)),
        ],
        compiler_params=pltpu.CompilerParams(vmem_limit_bytes=VMEM_BYTES),
        cost_estimate=pl.CostEstimate(
            flops=6 * slots * width * width,
            bytes_accessed=6 * width * width + 4 * slots * width,
            transcendentals=slots * width,
        ),
    )(rows, wide_all)


def exchange(rows, peer_count):
    parts = rows.reshape(peer_count, -1, rows.shape[1])
    return lax.all_to_all(parts, "exp", split_axis=0, concat_axis=0, tiled=True).reshape(rows.shape)


def gated_hidden(gate, upward):
    return (gate * jax.nn.sigmoid(1.702 * gate) * (upward + 1.0)).astype(jnp.bfloat16)


def attend(query_rows, key_value_rows, sinks):
    tokens_here = query_rows.shape[0]
    previous = shifted(key_value_rows, ("ctx", "exp"), 1)
    span_rows = WINDOW + tokens_here
    groups = QHEADS // KVHEADS
    span = jnp.concatenate([previous, key_value_rows], 0)
    all_keys = span[:, : KVHEADS * HEAD].reshape(span_rows, KVHEADS, HEAD)
    all_values = span[:, KVHEADS * HEAD :].reshape(span_rows, KVHEADS, HEAD)
    query_heads = query_rows.reshape(tokens_here, KVHEADS, groups, HEAD)
    scores = jnp.einsum(
        "ihgd,jhd->hgij", query_heads, all_keys, preferred_element_type=jnp.float32
    ) * (1.0 / math.sqrt(HEAD))
    first_row = lax.axis_index(("ctx", "exp")) * tokens_here
    query_place = first_row + jnp.arange(tokens_here, dtype=jnp.int32)
    key_place = first_row - WINDOW + jnp.arange(span_rows, dtype=jnp.int32)
    distance = query_place[:, None] - key_place[None, :]
    allowed = (distance >= 0) & (distance < WINDOW) & (key_place >= 0)[None, :]
    scores = jnp.where(allowed, scores, -1e30)
    sink_logit = sinks.reshape(KVHEADS, groups)[:, :, None]
    row_max = jnp.maximum(jnp.max(scores, -1), sink_logit)
    expo_terms = jnp.exp(scores - row_max[..., None])
    denom_total = jnp.sum(expo_terms, -1) + jnp.exp(sink_logit - row_max)
    probs = (expo_terms / denom_total[..., None]).astype(jnp.bfloat16)
    attended = jnp.einsum("hgij,jhd->ihgd", probs, all_values, preferred_element_type=jnp.float32)
    return attended.reshape(tokens_here, QHEADS * HEAD).astype(jnp.bfloat16)


def per_device(
    hidden_rows,
    queries,
    keys,
    values,
    sinks,
    norm_gain,
    learner_row,
    expert_ids,
    route_weight,
    gate_w,
    up_w,
    down_w,
):
    tokens_here = hidden_rows.shape[0]
    peer_count = lax.axis_size("exp")
    per_peer = tokens_here // peer_count
    gate_block, up_block, down_block = gate_w[0], up_w[0], down_w[0]

    depth, width = gate_block.shape
    wide = pack_call(gate_block, up_block, down_block)
    wide_all = lax.all_gather(wide, "ctx", axis=0, tiled=True)

    slot = learner_row % (peer_count * tokens_here) // tokens_here * per_peer + learner_row % per_peer
    order = (jnp.arange(tokens_here, dtype=jnp.int32)[:, None] == slot[None, :]).astype(jnp.bfloat16)
    resid = exchange(pick_rows(order, hidden_rows), peer_count)
    resid_float = resid.astype(jnp.float32)
    mean_square = jnp.mean(resid_float * resid_float, -1, keepdims=True)
    normed = (resid_float * lax.rsqrt(mean_square + 1e-05) * norm_gain).astype(jnp.bfloat16)

    slots_total = peer_count * CAP
    pair_count = tokens_here * ROUTES
    pair_expert = expert_ids.reshape(-1)
    hits = pair_expert[:, None] == jnp.arange(peer_count, dtype=jnp.int32)[None, :]
    pair_place = jnp.arange(pair_count, dtype=jnp.int32)
    before = (pair_place[:, None] > pair_place[None, :]).astype(jnp.bfloat16)
    earlier = jnp.dot(before, hits.astype(jnp.bfloat16), preferred_element_type=jnp.float32)
    pair_rank = jnp.sum(jnp.where(hits, earlier, 0.0), 1).astype(jnp.int32)
    slot_index = (pair_expert * CAP + pair_rank).reshape(tokens_here, ROUTES)
    slots = jnp.arange(slots_total, dtype=jnp.int32)
    sent = sum(slots[:, None] == slot_index[None, :, r] for r in range(ROUTES))
    outgoing = pick_rows(sent.astype(jnp.bfloat16), normed)
    expert_rows = exchange(outgoing, peer_count)
    packed = jnp.concatenate([queries, keys, values], 1)
    expert_rows, packed = lax.optimization_barrier((expert_rows, packed))
    spread_rows = spread_call(expert_rows, depth)
    arrived = exchange(pick_rows(order, packed), peer_count)
    query_rows = arrived[:, : QHEADS * HEAD]
    key_value_rows = arrived[:, QHEADS * HEAD :]
    weight_high = lax.reduce_precision(route_weight, 8, 7)
    weight_low = route_weight - weight_high

    def selection(weight):
        return sum(
            jnp.where(slots[None, :] == slot_index[:, r, None], weight[:, r, None], 0.0)
            for r in range(ROUTES)
        ).astype(jnp.bfloat16)

    combine = jnp.concatenate([selection(weight_high), selection(weight_low)], 0)

    attn_rows = attend(query_rows, key_value_rows, sinks)

    expert_out = experts_call(spread_rows, wide_all, depth, width)
    returned = exchange(expert_out, peer_count)
    both = jnp.dot(combine, returned, preferred_element_type=jnp.float32)
    total = both[:tokens_here] + both[tokens_here:]
    return (attn_rows, (resid_float + total).astype(jnp.bfloat16))


def solution(mesh):
    return jax.shard_map(
        per_device,
        mesh=mesh,
        in_specs=(
            P(("ctx", "exp"), None),
            P(("ctx", "exp"), None),
            P(("ctx", "exp"), None),
            P(("ctx", "exp"), None),
            P(),
            P(),
            P(("ctx", "exp")),
            P(("ctx", "exp"), None),
            P(("ctx", "exp"), None),
            P("exp", "ctx", None),
            P("exp", "ctx", None),
            P("exp", "ctx", None),
        ),
        out_specs=(P(("ctx", "exp"), None), P(("ctx", "exp"), None)),
        check_vma=False,
    )
```

```python
import math

import jax
import jax.numpy as jnp
from jax import lax
from jax.experimental import pallas as pl
from jax.experimental.pallas import tpu as pltpu
from jax.sharding import PartitionSpec as P

D = 1440
FFW = 1440
QHEADS = 32
KVHEADS = 4
HEAD = 64
WINDOW = 128
ROUTES = 2
CAP = 8
LANES = 128
ROWS = 8
VMEM_BYTES = 60 * 1024 * 1024


def shifted(block, axis, distance):
    devices = range(lax.axis_size(axis))
    route = [(i - distance, i) for i in devices if i - distance in devices]
    return lax.ppermute(block, axis, route)


def pick_rows(choice, rows):
    return jnp.dot(choice, rows, preferred_element_type=jnp.float32).astype(jnp.bfloat16)


def pitch_of(depth):
    return -(-depth // ROWS) * ROWS


def pack_kernel(gate_ref, up_ref, down_ref, packed_ref):
    depth, width = gate_ref.shape
    main = width // LANES * LANES
    left = width - main
    pitch, packed = packed_ref.shape
    packed_ref[depth:, :] = jnp.zeros((pitch - depth, packed), jnp.bfloat16)
    for place, ref in enumerate((gate_ref, up_ref, down_ref)):
        packed_ref[:depth, place * main : (place + 1) * main] = ref[:, :main]
        start = 3 * main + place * left
        packed_ref[:depth, start : start + left] = ref[:, main:]
    packed_ref[:depth, 3 * width :] = jnp.zeros((depth, packed - 3 * width), jnp.bfloat16)


def pack_call(gate_block, up_block, down_block):
    depth, width = gate_block.shape
    packed = 3 * (width // LANES) * LANES + LANES
    return pl.pallas_call(
        pack_kernel,
        out_shape=jax.ShapeDtypeStruct((pitch_of(depth), packed), jnp.bfloat16),
        cost_estimate=pl.CostEstimate(
            flops=0, bytes_accessed=12 * depth * width, transcendentals=0
        ),
    )(gate_block, up_block, down_block)


def spread(source, target, depth):
    pitch = pitch_of(depth)
    for s in range(source.shape[1] // depth):
        target[:, s * pitch : s * pitch + depth] = source[:, s * depth : (s + 1) * depth]
        target[:, s * pitch + depth : (s + 1) * pitch] = jnp.zeros(
            (source.shape[0], pitch - depth), jnp.bfloat16
        )


def spread_call(rows, depth):
    slots, width = rows.shape

    def spread_kernel(rows_ref, spread_ref):
        spread(rows_ref, spread_ref, depth)

    return pl.pallas_call(
        spread_kernel,
        out_shape=jax.ShapeDtypeStruct((slots, width // depth * pitch_of(depth)), jnp.bfloat16),
        cost_estimate=pl.CostEstimate(
            flops=0, bytes_accessed=4 * slots * width, transcendentals=0
        ),
    )(rows)


def experts_kernel(depth, rows_ref, wide_ref, out_ref, rows, wide, again, arrival):
    slots, width = out_ref.shape
    packed = wide_ref.shape[1]
    main = width // LANES * LANES
    left = width - main
    pitch = pitch_of(depth)
    step = 2 * LANES
    cuts = [(low, min(low + step, main)) for low in range(0, main, step)]
    copies = []

    def fetch(source, target):
        copies.append(pltpu.make_async_copy(source, target, arrival.at[len(copies)]))
        copies[-1].start()

    def fetch_columns(low, high):
        piece = (slice(None), pl.ds(low, high - low))
        fetch(wide_ref.at[piece], wide.at[piece])

    fetch(rows_ref, rows)
    for low, high in cuts:
        fetch_columns(low, high)
        fetch_columns(main + low, main + high)
    fetch_columns(2 * main, packed)
    for s in range(width // depth):
        again[:, s * pitch + depth : (s + 1) * pitch] = jnp.zeros(
            (slots, pitch - depth), jnp.bfloat16
        )

    def keep(activ, low):
        high = low + activ.shape[1]
        for s in range(low // depth, -(-high // depth)):
            first, last = max(low, s * depth), min(high, (s + 1) * depth)
            place = s * (pitch - depth)
            again[:, first + place : last + place] = activ[:, first - low : last - low]

    copies[0].wait()
    for place, (low, high) in enumerate(cuts):
        copies[2 * place + 1].wait()
        copies[2 * place + 2].wait()
        parts = [wide[:, low:high], wide[:, main + low : main + high]]
        span = high - low
        if high == main:
            copies[-1].wait()
            parts.append(wide[:, 3 * main :])
        both = jnp.dot(
            rows[...], jnp.concatenate(parts, 1), preferred_element_type=jnp.float32
        )
        keep(gated_hidden(both[:, :span], both[:, span : 2 * span]), low)
        if high == main:
            rest = both[:, 2 * span :]
            keep(gated_hidden(rest[:, :left], rest[:, left : 2 * left]), main)

    wider = 2 * step
    for low in range(0, main, wider):
        high = min(low + wider, packed - 2 * main)
        total = jnp.dot(
            again[...],
            wide[:, 2 * main + low : 2 * main + high],
            preferred_element_type=jnp.float32,
        ).astype(jnp.bfloat16)
        end = min(high, main)
        out_ref[:, low:end] = total[:, : end - low]
        if high > main:
            tail = main - low + 2 * left
            out_ref[:, main:] = total[:, tail : tail + left]


def experts_call(rows, wide_all, depth, width):
    slots = rows.shape[0]
    distant = pl.BlockSpec(memory_space=pltpu.HBM)
    tiles = -(-(width // LANES) // 2)

    def kernel(*refs):
        experts_kernel(depth, *refs)

    return pl.pallas_call(
        kernel,
        out_shape=jax.ShapeDtypeStruct((slots, width), jnp.bfloat16),
        in_specs=[distant, distant],
        out_specs=pl.BlockSpec(memory_space=pltpu.VMEM),
        scratch_shapes=[
            pltpu.VMEM(rows.shape, jnp.bfloat16),
            pltpu.VMEM(wide_all.shape, jnp.bfloat16),
            pltpu.VMEM(rows.shape, jnp.bfloat16),
            pltpu.SemaphoreType.DMA((2 * tiles + 2,)),
        ],
        compiler_params=pltpu.CompilerParams(vmem_limit_bytes=VMEM_BYTES),
        cost_estimate=pl.CostEstimate(
            flops=6 * slots * width * width,
            bytes_accessed=6 * width * width + 4 * slots * width,
            transcendentals=slots * width,
        ),
    )(rows, wide_all)


def exchange(rows, peer_count):
    parts = rows.reshape(peer_count, -1, rows.shape[1])
    return lax.all_to_all(parts, "exp", split_axis=0, concat_axis=0, tiled=True).reshape(rows.shape)


def gated_hidden(gate, upward):
    return (gate * jax.nn.sigmoid(1.702 * gate) * (upward + 1.0)).astype(jnp.bfloat16)


def attend(query_rows, key_value_rows, sinks):
    tokens_here = query_rows.shape[0]
    previous = shifted(key_value_rows, ("ctx", "exp"), 1)
    span_rows = WINDOW + tokens_here
    groups = QHEADS // KVHEADS
    span = jnp.concatenate([previous, key_value_rows], 0)
    all_keys = span[:, : KVHEADS * HEAD].reshape(span_rows, KVHEADS, HEAD)
    all_values = span[:, KVHEADS * HEAD :].reshape(span_rows, KVHEADS, HEAD)
    query_heads = query_rows.reshape(tokens_here, KVHEADS, groups, HEAD)
    scores = jnp.einsum(
        "ihgd,jhd->hgij", query_heads, all_keys, preferred_element_type=jnp.float32
    ) * (1.0 / math.sqrt(HEAD))
    first_row = lax.axis_index(("ctx", "exp")) * tokens_here
    query_place = first_row + jnp.arange(tokens_here, dtype=jnp.int32)
    key_place = first_row - WINDOW + jnp.arange(span_rows, dtype=jnp.int32)
    distance = query_place[:, None] - key_place[None, :]
    allowed = (distance >= 0) & (distance < WINDOW) & (key_place >= 0)[None, :]
    scores = jnp.where(allowed, scores, -1e30)
    sink_logit = sinks.reshape(KVHEADS, groups)[:, :, None]
    row_max = jnp.maximum(jnp.max(scores, -1), sink_logit)
    expo_terms = jnp.exp(scores - row_max[..., None])
    denom_total = jnp.sum(expo_terms, -1) + jnp.exp(sink_logit - row_max)
    probs = (expo_terms / denom_total[..., None]).astype(jnp.bfloat16)
    attended = jnp.einsum("hgij,jhd->ihgd", probs, all_values, preferred_element_type=jnp.float32)
    return attended.reshape(tokens_here, QHEADS * HEAD).astype(jnp.bfloat16)


def per_device(
    hidden_rows,
    queries,
    keys,
    values,
    sinks,
    norm_gain,
    learner_row,
    expert_ids,
    route_weight,
    gate_w,
    up_w,
    down_w,
):
    tokens_here = hidden_rows.shape[0]
    peer_count = lax.axis_size("exp")
    per_peer = tokens_here // peer_count
    gate_block, up_block, down_block = gate_w[0], up_w[0], down_w[0]

    depth, width = gate_block.shape
    wide = pack_call(gate_block, up_block, down_block)
    wide_all = lax.all_gather(wide, "ctx", axis=0, tiled=True)

    slot = learner_row % (peer_count * tokens_here) // tokens_here * per_peer + learner_row % per_peer
    order = (jnp.arange(tokens_here, dtype=jnp.int32)[:, None] == slot[None, :]).astype(jnp.bfloat16)
    resid = exchange(pick_rows(order, hidden_rows), peer_count)
    resid_float = resid.astype(jnp.float32)
    mean_square = jnp.mean(resid_float * resid_float, -1, keepdims=True)
    normed = (resid_float * lax.rsqrt(mean_square + 1e-05) * norm_gain).astype(jnp.bfloat16)

    slots_total = peer_count * CAP
    pair_count = tokens_here * ROUTES
    pair_expert = expert_ids.reshape(-1)
    hits = pair_expert[:, None] == jnp.arange(peer_count, dtype=jnp.int32)[None, :]
    pair_place = jnp.arange(pair_count, dtype=jnp.int32)
    before = (pair_place[:, None] > pair_place[None, :]).astype(jnp.bfloat16)
    earlier = jnp.dot(before, hits.astype(jnp.bfloat16), preferred_element_type=jnp.float32)
    pair_rank = jnp.sum(jnp.where(hits, earlier, 0.0), 1).astype(jnp.int32)
    slot_index = (pair_expert * CAP + pair_rank).reshape(tokens_here, ROUTES)
    slots = jnp.arange(slots_total, dtype=jnp.int32)
    sent = sum(slots[:, None] == slot_index[None, :, r] for r in range(ROUTES))
    outgoing = pick_rows(sent.astype(jnp.bfloat16), normed)
    expert_rows = exchange(outgoing, peer_count)
    packed = jnp.concatenate([queries, keys, values], 1)
    expert_rows, packed = lax.optimization_barrier((expert_rows, packed))
    spread_rows = spread_call(expert_rows, depth)
    arrived = exchange(pick_rows(order, packed), peer_count)
    query_rows = arrived[:, : QHEADS * HEAD]
    key_value_rows = arrived[:, QHEADS * HEAD :]
    weight_high = lax.reduce_precision(route_weight, 8, 7)
    weight_low = route_weight - weight_high

    def selection(weight):
        return sum(
            jnp.where(slots[None, :] == slot_index[:, r, None], weight[:, r, None], 0.0)
            for r in range(ROUTES)
        ).astype(jnp.bfloat16)

    combine = jnp.concatenate([selection(weight_high), selection(weight_low)], 0)

    attn_rows = attend(query_rows, key_value_rows, sinks)

    expert_out = experts_call(spread_rows, wide_all, depth, width)
    returned = exchange(expert_out, peer_count)
    both = jnp.dot(combine, returned, preferred_element_type=jnp.float32)
    total = both[:tokens_here] + both[tokens_here:]
    return (attn_rows, (resid_float + total).astype(jnp.bfloat16))


def solution(mesh):
    return jax.shard_map(
        per_device,
        mesh=mesh,
        in_specs=(
            P(("ctx", "exp"), None),
            P(("ctx", "exp"), None),
            P(("ctx", "exp"), None),
            P(("ctx", "exp"), None),
            P(),
            P(),
            P(("ctx", "exp")),
            P(("ctx", "exp"), None),
            P(("ctx", "exp"), None),
            P("exp", "ctx", None),
            P("exp", "ctx", None),
            P("exp", "ctx", None),
        ),
        out_specs=(P(("ctx", "exp"), None), P(("ctx", "exp"), None)),
        check_vma=False,
    )
```

```python
import math

import jax
import jax.numpy as jnp
from jax import lax
from jax.experimental import pallas as pl
from jax.experimental.pallas import tpu as pltpu
from jax.sharding import PartitionSpec as P

D = 1440
FFW = 1440
QHEADS = 32
KVHEADS = 4
HEAD = 64
WINDOW = 128
ROUTES = 2
CAP = 8
LANES = 128
ROWS = 8
VMEM_BYTES = 60 * 1024 * 1024


def shifted(block, axis, distance):
    devices = range(lax.axis_size(axis))
    route = [(i - distance, i) for i in devices if i - distance in devices]
    return lax.ppermute(block, axis, route)


def pick_rows(choice, rows):
    return jnp.dot(choice, rows, preferred_element_type=jnp.float32).astype(jnp.bfloat16)


def pitch_of(depth):
    return -(-depth // ROWS) * ROWS


def pack_kernel(gate_ref, up_ref, down_ref, packed_ref):
    depth, width = gate_ref.shape
    main = width // LANES * LANES
    left = width - main
    pitch, packed = packed_ref.shape
    packed_ref[depth:, :] = jnp.zeros((pitch - depth, packed), jnp.bfloat16)
    for place, ref in enumerate((gate_ref, up_ref, down_ref)):
        packed_ref[:depth, place * main : (place + 1) * main] = ref[:, :main]
        start = 3 * main + place * left
        packed_ref[:depth, start : start + left] = ref[:, main:]
    packed_ref[:depth, 3 * width :] = jnp.zeros((depth, packed - 3 * width), jnp.bfloat16)


def pack_call(gate_block, up_block, down_block):
    depth, width = gate_block.shape
    packed = 3 * (width // LANES) * LANES + LANES
    return pl.pallas_call(
        pack_kernel,
        out_shape=jax.ShapeDtypeStruct((pitch_of(depth), packed), jnp.bfloat16),
        cost_estimate=pl.CostEstimate(
            flops=0, bytes_accessed=12 * depth * width, transcendentals=0
        ),
    )(gate_block, up_block, down_block)


def spread(source, target, depth):
    pitch = pitch_of(depth)
    for s in range(source.shape[1] // depth):
        target[:, s * pitch : s * pitch + depth] = source[:, s * depth : (s + 1) * depth]
        target[:, s * pitch + depth : (s + 1) * pitch] = jnp.zeros(
            (source.shape[0], pitch - depth), jnp.bfloat16
        )


def spread_call(rows, depth):
    slots, width = rows.shape

    def spread_kernel(rows_ref, spread_ref):
        spread(rows_ref, spread_ref, depth)

    return pl.pallas_call(
        spread_kernel,
        out_shape=jax.ShapeDtypeStruct((slots, width // depth * pitch_of(depth)), jnp.bfloat16),
        cost_estimate=pl.CostEstimate(
            flops=0, bytes_accessed=4 * slots * width, transcendentals=0
        ),
    )(rows)


def experts_kernel(depth, rows_ref, wide_ref, out_ref, rows, wide, again, arrival):
    slots, width = out_ref.shape
    packed = wide_ref.shape[1]
    main = width // LANES * LANES
    left = width - main
    pitch = pitch_of(depth)
    step = 2 * LANES
    lead = main % step
    cuts = [(max(low, 0), low + step) for low in range(lead - step, main, step)]
    copies = []

    def fetch(source, target):
        copies.append(pltpu.make_async_copy(source, target, arrival.at[len(copies)]))
        copies[-1].start()

    def fetch_columns(low, high):
        piece = (slice(None), pl.ds(low, high - low))
        fetch(wide_ref.at[piece], wide.at[piece])

    fetch(rows_ref, rows)
    for low, high in cuts:
        fetch_columns(low, high)
        fetch_columns(main + low, main + high)
    fetch_columns(2 * main, packed)
    for s in range(width // depth):
        again[:, s * pitch + depth : (s + 1) * pitch] = jnp.zeros(
            (slots, pitch - depth), jnp.bfloat16
        )

    def keep(activ, low):
        high = low + activ.shape[1]
        for s in range(low // depth, -(-high // depth)):
            first, last = max(low, s * depth), min(high, (s + 1) * depth)
            place = s * (pitch - depth)
            again[:, first + place : last + place] = activ[:, first - low : last - low]

    copies[0].wait()
    for place, (low, high) in enumerate(cuts):
        copies[2 * place + 1].wait()
        copies[2 * place + 2].wait()
        parts = [wide[:, low:high], wide[:, main + low : main + high]]
        span = high - low
        if high == main:
            copies[-1].wait()
            parts.append(wide[:, 3 * main :])
        both = jnp.dot(
            rows[...], jnp.concatenate(parts, 1), preferred_element_type=jnp.float32
        )
        keep(gated_hidden(both[:, :span], both[:, span : 2 * span]), low)
        if high == main:
            rest = both[:, 2 * span :]
            keep(gated_hidden(rest[:, :left], rest[:, left : 2 * left]), main)

    wider = 2 * step
    for low in range(0, main, wider):
        high = min(low + wider, packed - 2 * main)
        total = jnp.dot(
            again[...],
            wide[:, 2 * main + low : 2 * main + high],
            preferred_element_type=jnp.float32,
        ).astype(jnp.bfloat16)
        end = min(high, main)
        out_ref[:, low:end] = total[:, : end - low]
        if high > main:
            tail = main - low + 2 * left
            out_ref[:, main:] = total[:, tail : tail + left]


def experts_call(rows, wide_all, depth, width):
    slots = rows.shape[0]
    distant = pl.BlockSpec(memory_space=pltpu.HBM)
    tiles = width // LANES // 2 + 1

    def kernel(*refs):
        experts_kernel(depth, *refs)

    return pl.pallas_call(
        kernel,
        out_shape=jax.ShapeDtypeStruct((slots, width), jnp.bfloat16),
        in_specs=[distant, distant],
        out_specs=pl.BlockSpec(memory_space=pltpu.VMEM),
        scratch_shapes=[
            pltpu.VMEM(rows.shape, jnp.bfloat16),
            pltpu.VMEM(wide_all.shape, jnp.bfloat16),
            pltpu.VMEM(rows.shape, jnp.bfloat16),
            pltpu.SemaphoreType.DMA((2 * tiles + 2,)),
        ],
        compiler_params=pltpu.CompilerParams(vmem_limit_bytes=VMEM_BYTES),
        cost_estimate=pl.CostEstimate(
            flops=6 * slots * width * width,
            bytes_accessed=6 * width * width + 4 * slots * width,
            transcendentals=slots * width,
        ),
    )(rows, wide_all)


def exchange(rows, peer_count):
    parts = rows.reshape(peer_count, -1, rows.shape[1])
    return lax.all_to_all(parts, "exp", split_axis=0, concat_axis=0, tiled=True).reshape(rows.shape)


def gated_hidden(gate, upward):
    return (gate * (0.5 + 0.5 * jnp.tanh(0.851 * gate)) * (upward + 1.0)).astype(jnp.bfloat16)


def attend(query_rows, key_value_rows, sinks):
    tokens_here = query_rows.shape[0]
    previous = shifted(key_value_rows, ("ctx", "exp"), 1)
    span_rows = WINDOW + tokens_here
    groups = QHEADS // KVHEADS
    span = jnp.concatenate([previous, key_value_rows], 0)
    all_keys = span[:, : KVHEADS * HEAD].reshape(span_rows, KVHEADS, HEAD)
    all_values = span[:, KVHEADS * HEAD :].reshape(span_rows, KVHEADS, HEAD)
    query_heads = query_rows.reshape(tokens_here, KVHEADS, groups, HEAD)
    scores = jnp.einsum(
        "ihgd,jhd->hgij", query_heads, all_keys, preferred_element_type=jnp.float32
    ) * (1.0 / math.sqrt(HEAD))
    first_row = lax.axis_index(("ctx", "exp")) * tokens_here
    query_place = first_row + jnp.arange(tokens_here, dtype=jnp.int32)
    key_place = first_row - WINDOW + jnp.arange(span_rows, dtype=jnp.int32)
    distance = query_place[:, None] - key_place[None, :]
    allowed = (distance >= 0) & (distance < WINDOW) & (key_place >= 0)[None, :]
    scores = jnp.where(allowed, scores, -1e30)
    sink_logit = sinks.reshape(KVHEADS, groups)[:, :, None]
    row_max = jnp.maximum(jnp.max(scores, -1), sink_logit)
    expo_terms = jnp.exp(scores - row_max[..., None])
    denom_total = jnp.sum(expo_terms, -1) + jnp.exp(sink_logit - row_max)
    probs = (expo_terms / denom_total[..., None]).astype(jnp.bfloat16)
    attended = jnp.einsum("hgij,jhd->ihgd", probs, all_values, preferred_element_type=jnp.float32)
    return attended.reshape(tokens_here, QHEADS * HEAD).astype(jnp.bfloat16)


def per_device(
    hidden_rows,
    queries,
    keys,
    values,
    sinks,
    norm_gain,
    learner_row,
    expert_ids,
    route_weight,
    gate_w,
    up_w,
    down_w,
):
    tokens_here = hidden_rows.shape[0]
    peer_count = lax.axis_size("exp")
    per_peer = tokens_here // peer_count
    gate_block, up_block, down_block = gate_w[0], up_w[0], down_w[0]

    depth, width = gate_block.shape
    wide = pack_call(gate_block, up_block, down_block)
    wide_all = lax.all_gather(wide, "ctx", axis=0, tiled=True)

    slot = learner_row % (peer_count * tokens_here) // tokens_here * per_peer + learner_row % per_peer
    order = (jnp.arange(tokens_here, dtype=jnp.int32)[:, None] == slot[None, :]).astype(jnp.bfloat16)
    resid = exchange(pick_rows(order, hidden_rows), peer_count)
    resid_float = resid.astype(jnp.float32)
    mean_square = jnp.mean(resid_float * resid_float, -1, keepdims=True)
    normed = (resid_float * lax.rsqrt(mean_square + 1e-05) * norm_gain).astype(jnp.bfloat16)

    slots_total = peer_count * CAP
    pair_count = tokens_here * ROUTES
    pair_expert = expert_ids.reshape(-1)
    hits = pair_expert[:, None] == jnp.arange(peer_count, dtype=jnp.int32)[None, :]
    pair_place = jnp.arange(pair_count, dtype=jnp.int32)
    before = (pair_place[:, None] > pair_place[None, :]).astype(jnp.bfloat16)
    earlier = jnp.dot(before, hits.astype(jnp.bfloat16), preferred_element_type=jnp.float32)
    pair_rank = jnp.sum(jnp.where(hits, earlier, 0.0), 1).astype(jnp.int32)
    slot_index = (pair_expert * CAP + pair_rank).reshape(tokens_here, ROUTES)
    slots = jnp.arange(slots_total, dtype=jnp.int32)
    sent = sum(slots[:, None] == slot_index[None, :, r] for r in range(ROUTES))
    outgoing = pick_rows(sent.astype(jnp.bfloat16), normed)
    expert_rows = exchange(outgoing, peer_count)
    packed = jnp.concatenate([queries, keys, values], 1)
    expert_rows, packed = lax.optimization_barrier((expert_rows, packed))
    spread_rows = spread_call(expert_rows, depth)
    arrived = exchange(pick_rows(order, packed), peer_count)
    query_rows = arrived[:, : QHEADS * HEAD]
    key_value_rows = arrived[:, QHEADS * HEAD :]
    weight_high = lax.reduce_precision(route_weight, 8, 7)
    weight_low = route_weight - weight_high

    def selection(weight):
        return sum(
            jnp.where(slots[None, :] == slot_index[:, r, None], weight[:, r, None], 0.0)
            for r in range(ROUTES)
        ).astype(jnp.bfloat16)

    combine = jnp.concatenate([selection(weight_high), selection(weight_low)], 0)

    attn_rows = attend(query_rows, key_value_rows, sinks)

    expert_out = experts_call(spread_rows, wide_all, depth, width)
    returned = exchange(expert_out, peer_count)
    both = jnp.dot(combine, returned, preferred_element_type=jnp.float32)
    total = both[:tokens_here] + both[tokens_here:]
    return (attn_rows, (resid_float + total).astype(jnp.bfloat16))


def solution(mesh):
    return jax.shard_map(
        per_device,
        mesh=mesh,
        in_specs=(
            P(("ctx", "exp"), None),
            P(("ctx", "exp"), None),
            P(("ctx", "exp"), None),
            P(("ctx", "exp"), None),
            P(),
            P(),
            P(("ctx", "exp")),
            P(("ctx", "exp"), None),
            P(("ctx", "exp"), None),
            P("exp", "ctx", None),
            P("exp", "ctx", None),
            P("exp", "ctx", None),
        ),
        out_specs=(P(("ctx", "exp"), None), P(("ctx", "exp"), None)),
        check_vma=False,
    )
```
